32 devices in a mesh: enc: 4 (over y, core), seq: 8 (over z, x).
Axes of the slice: x: 2, y: 2, z: 4, core: 2. Of those that a mesh axis runs over, the one named last changes fastest.
Arguments:
- hidden: bfloat16 [2048, 4096], P('seq'), may hold values from -6 to 6
- dec_gain: float32 [4096], replicated, may hold values from 0.1 to 1.9
- cca_query: bfloat16 [4096, 4096], P(None, 'enc'), may hold values from -0.5 to 0.5
- cca_key: bfloat16 [896, 4096], P(None, 'enc'), may hold values from -0.5 to 0.5
- cca_value: bfloat16 [896, 4096], P(None, 'enc'), may hold values from -0.1875 to 0.1875
- cca_out: bfloat16 [4096, 4096], P('enc'), may hold values from -0.09375 to 0.09375
- neighbours: bfloat16 [8, 8, 128, 896], P('seq', 'enc'), may hold values from -6 to 6
- enc_gain: float32 [896], replicated, may hold values from 0.1 to 1.9
- enc_query: bfloat16 [896, 896], P('enc'), may hold values from -0.5 to 0.5
- enc_key: bfloat16 [896, 896], P('enc'), may hold values from -0.5 to 0.5
- enc_value: bfloat16 [896, 896], P('enc'), may hold values from -0.1875 to 0.1875
- enc_output: bfloat16 [896, 896], P('enc'), may hold values from -0.1875 to 0.1875
- enc_cotangent: bfloat16 [8, 8, 128, 896], P('seq', 'enc'), may hold values from -6 to 6
- neighbour_ids: int32 [32, 2], P('seq'), may hold values from 0 to 7, as said below
Outputs:
- mixed: bfloat16 [2048, 4096], P('seq', 'enc')
- d_neighbours: bfloat16 [8, 8, 128, 896], P('seq', 'enc')
- grad_query: float32 [896, 896], P(('enc', 'seq'))
- grad_key: float32 [896, 896], P(('enc', 'seq'))
- grad_value: float32 [896, 896], P(('enc', 'seq'))
- grad_out: float32 [896, 896], P(('enc', 'seq'))
The draws below stay inside these ranges and needn't reach their ends.
Inputs may be any that keep to these rules, and one draw needn't show every extreme that they name: `neighbour_ids`: within each aligned block of 4 stretches every position 0 to 7 appears exactly once.
All inputs are finite; a program needn't handle non-finite values.
Results may differ from the reference program's by a relative error of at most 0.025.
Values may be sent and summed in bfloat16 or wider, within the bound.
A program may use at most 192 MiB of HBM per device.

```python
import math
import jax
import jax.numpy as jnp
from jax import lax

D = 4096
HD = 128
DE = 896
EHEADS = 14
EHD = 64
C = 64
R = 128
K = 2
SEQ_LEN = 2048
CH_DEV = 4
TOK_DEV = 256
COLUMNS = 8
STRETCHES = 32
TOKENS = 2048


def pair_draw(key):
    key_base, key_other = jax.random.split(jax.random.fold_in(key, 31), 2)
    base_draw = jnp.clip(jax.random.normal(key_base, (DE, DE), jnp.float32), -6.0, 6.0) / math.sqrt(DE)
    other_draw = jnp.clip(jax.random.normal(key_other, (DE, DE), jnp.float32), -6.0, 6.0) / math.sqrt(DE)
    first_out = base_draw
    second_out = other_draw
    return (jnp.clip(first_out, -0.5, 0.5), jnp.clip(second_out, -0.5, 0.5))


def draw_enc_query(key, part):
    return pair_draw(key)[0].astype(jnp.bfloat16)


def draw_enc_key(key, part):
    return pair_draw(key)[1].astype(jnp.bfloat16)


def draw_cca_query(key, part):
    base_draw = jnp.clip(jax.random.normal(jax.random.fold_in(key, 53), (D, D), jnp.float32), -6.0, 6.0) / math.sqrt(D)
    return jnp.clip(base_draw, -0.5, 0.5).astype(jnp.bfloat16)


def draw_cca_key(key, part):
    base_draw = jnp.clip(jax.random.normal(jax.random.fold_in(key, 59), (DE, D), jnp.float32), -6.0, 6.0) / math.sqrt(DE)
    return jnp.clip(base_draw, -0.5, 0.5).astype(jnp.bfloat16)


def draw_neighbour_ids(key, part):
    block_keys = jax.random.split(jax.random.fold_in(key, 5), STRETCHES // CH_DEV)
    blocks = jax.vmap(lambda block_key: jax.random.permutation(block_key, CH_DEV * K))(block_keys)
    return blocks.reshape(STRETCHES, K).astype(jnp.int32)


def block_levels(own_key, extent, cuts, smallest, high):
    def one(dim, shards_of):
        draws = jax.random.uniform(jax.random.fold_in(jax.random.fold_in(own_key, 6), dim), (shards_of,), jnp.float32, smallest / len(cuts), high / len(cuts))
        return jnp.repeat(jnp.exp(draws), extent[dim] // shards_of).reshape((-1,) + (1,) * (len(extent) - dim - 1))

    gain = one(*cuts[0])
    for cut in cuts[1:]:
        gain = gain * one(*cut)
    return gain


def bell_draw(key, dims, scale, most, shards=(), kind=jnp.bfloat16):
    array = jax.random.normal(key, dims, jnp.float32) * scale
    if len(shards) > 0:
        array = block_levels(key, dims, shards, -0.22, 0.18) * array
    return jnp.clip(array, min=-most, max=most).astype(kind)


def setup_inputs(seed: int = 0) -> dict:
    streams_of = jax.random.split(jax.random.key(seed), 15)
    hidden = bell_draw(streams_of[0], (TOKENS, D), 1.0, 6.0, ((0, 8),))
    dec_gain = jnp.clip(1.0 + 0.18 * jax.random.normal(streams_of[1], (D,), jnp.float32), 0.1, 1.9)
    cca_query = draw_cca_query(jax.random.fold_in(streams_of[14], 71), 0)
    cca_key = draw_cca_key(jax.random.fold_in(streams_of[14], 71), 0)
    cca_value = bell_draw(streams_of[4], (DE, D), DE ** -0.5, 0.1875, ((1, 4),))
    cca_out = bell_draw(streams_of[5], (D, D), D ** -0.5, 0.09375, ((0, 4),))
    neighbours = bell_draw(streams_of[6], (COLUMNS, CH_DEV * K, R, DE), 1.0, 6.0, ((0, 8), (1, 4)))
    enc_gain = jnp.clip(1.0 + 0.18 * jax.random.normal(streams_of[7], (DE,), jnp.float32), 0.1, 1.9)
    enc_query = draw_enc_query(jax.random.fold_in(streams_of[14], 71), 0)
    enc_key = draw_enc_key(jax.random.fold_in(streams_of[14], 71), 0)
    enc_value = bell_draw(streams_of[10], (DE, DE), DE ** -0.5, 0.1875, ((0, 4),))
    enc_output = bell_draw(streams_of[11], (DE, DE), DE ** -0.5, 0.1875, ((0, 4),))
    enc_cotangent = bell_draw(streams_of[12], (COLUMNS, CH_DEV * K, R, DE), 1.0, 6.0, ((0, 8), (1, 4)))
    neighbour_ids = draw_neighbour_ids(jax.random.fold_in(streams_of[14], 71), 0)
    return {"hidden": hidden, "dec_gain": dec_gain, "cca_query": cca_query, "cca_key": cca_key, "cca_value": cca_value, "cca_out": cca_out, "neighbours": neighbours, "enc_gain": enc_gain, "enc_query": enc_query, "enc_key": enc_key, "enc_value": enc_value, "enc_output": enc_output, "enc_cotangent": enc_cotangent, "neighbour_ids": neighbour_ids}


EPS = 1e-06

def batched(pattern, former, latter):
    return jnp.einsum(pattern, former.astype(jnp.float32), latter.astype(jnp.float32))

def matmul(former, latter):
    return jnp.dot(former, latter, preferred_element_type=jnp.float32)

def inner_rows(former, latter):
    return lax.dot_general(former, latter, (((0,), (0,)), ((), ())), preferred_element_type=jnp.float32)

def outer_cols(former, latter):
    return lax.dot_general(former, latter, (((1,), (1,)), ((), ())), preferred_element_type=jnp.float32)

def encode(rows_in, gain_vec, matrices, pieces):
    w_query, w_key, w_value, w_output = matrices
    x_float = rows_in.astype(jnp.float32)
    inv_rms = lax.rsqrt(lax.optimization_barrier(jnp.mean(x_float * x_float, axis=-1, keepdims=True)) + EPS)
    normed = (x_float * inv_rms * gain_vec).astype(jnp.bfloat16)
    layout = (pieces, R, EHEADS, EHD)
    queries = matmul(normed, w_query).astype(jnp.bfloat16).reshape(layout)
    keys_all = matmul(normed, w_key).astype(jnp.bfloat16).reshape(layout)
    values_all = matmul(normed, w_value).astype(jnp.bfloat16).reshape(layout)
    scores = batched('nqhd,nkhd->nhqk', queries, keys_all) * EHD ** (-0.5)
    soft_max = jax.nn.softmax(scores, axis=-1)
    soft_low = soft_max.astype(jnp.bfloat16)
    context = batched('nhqk,nkhd->nqhd', soft_low, values_all).astype(jnp.bfloat16).reshape(pieces * R, DE)
    encoded = (x_float + matmul(context, w_output)).astype(jnp.bfloat16)
    return (encoded, (x_float, inv_rms, normed, queries, keys_all, values_all, soft_max, soft_low, context))

def encode_backward(cotangent, saved, matrices, gain_vec, pieces):
    w_query, w_key, w_value, w_output = matrices
    x_float, inv_rms, normed, queries, keys_all, values_all, soft_max, soft_low, context = saved
    layout = (pieces, R, EHEADS, EHD)
    grad_output = inner_rows(context, cotangent)
    d_context = outer_cols(cotangent, w_output).astype(jnp.bfloat16).reshape(layout)
    d_soft = batched('nqhd,nkhd->nhqk', d_context, values_all)
    d_values = batched('nhqk,nqhd->nkhd', soft_low, d_context).astype(jnp.bfloat16).reshape(pieces * R, DE)
    d_scores = (soft_max * (d_soft - lax.optimization_barrier(jnp.sum(d_soft * soft_max, axis=-1, keepdims=True))) * EHD ** (-0.5)).astype(jnp.bfloat16)
    d_queries = batched('nhqk,nkhd->nqhd', d_scores, keys_all).astype(jnp.bfloat16).reshape(pieces * R, DE)
    d_keys = batched('nhqk,nqhd->nkhd', d_scores, queries).astype(jnp.bfloat16).reshape(pieces * R, DE)
    grad_query = inner_rows(normed, d_queries)
    grad_key = inner_rows(normed, d_keys)
    grad_value = inner_rows(normed, d_values)
    d_normed = outer_cols(d_queries, w_query) + outer_cols(d_keys, w_key) + outer_cols(d_values, w_value)
    scaled = d_normed * gain_vec
    d_rows = inv_rms * scaled - x_float * inv_rms ** 3 * lax.optimization_barrier(jnp.mean(x_float * scaled, axis=-1, keepdims=True))
    d_input = (cotangent.astype(jnp.float32) + d_rows).astype(jnp.bfloat16)
    return (d_input, (grad_query, grad_key, grad_value, grad_output))

def attend(grouped, pairs):
    group_count, span_rows, width_here = grouped.shape
    heads_here = width_here // HD
    key_rows = pairs.shape[1]
    split_q = grouped.reshape(group_count, span_rows, heads_here, HD)
    split_k = pairs[..., :width_here].reshape(group_count, key_rows, heads_here, HD)
    split_v = pairs[..., width_here:].reshape(group_count, key_rows, heads_here, HD)
    scores = batched('gqhd,gkhd->ghqk', split_q, split_k) * HD ** (-0.5)
    soft_max = jax.nn.softmax(scores, axis=-1)
    soft_low = soft_max.astype(jnp.bfloat16)
    return batched('ghqk,gkhd->gqhd', soft_low, split_v).astype(jnp.bfloat16).reshape(group_count * span_rows, width_here)

def reference(hidden, dec_gain, cca_query, cca_key, cca_value, cca_out, neighbours, enc_gain, enc_query, enc_key, enc_value, enc_output, enc_cotangent, neighbour_ids):
    pieces = COLUMNS * CH_DEV * K
    matrices = (enc_query, enc_key, enc_value, enc_output)
    encoded, saved = encode(neighbours.reshape(pieces * R, DE), enc_gain, matrices, pieces)
    d_input, partials = encode_backward(enc_cotangent.reshape(pieces * R, DE), saved, matrices, enc_gain, pieces)
    grads = tuple((partial_sum / pieces for partial_sum in partials))
    groups_all = encoded.reshape(COLUMNS, CH_DEV * K, R, DE)
    id_blocks = neighbour_ids.reshape(COLUMNS, CH_DEV, K).astype(jnp.int32)
    last_rows = jax.vmap(lambda group_rows, chosen: jnp.take(group_rows, chosen, axis=0))(groups_all, id_blocks[:, CH_DEV - 1, :])
    earlier_all = jnp.concatenate([jnp.zeros_like(last_rows[:1]), last_rows[:-1]], axis=0)
    pair_weight = jnp.concatenate([cca_key, cca_value], axis=1)
    blocks = hidden.reshape(COLUMNS, TOK_DEV, D)

    def one_column(packed):
        block_rows, column_rows, chosen, earlier, column_index = packed
        key_value = matmul(column_rows.reshape(CH_DEV * K * R, DE), pair_weight).astype(jnp.bfloat16).reshape(CH_DEV * K, R, 2 * D)
        own_pairs = jnp.take(key_value, chosen, axis=0).reshape(CH_DEV, K * R, 2 * D)
        before = matmul(earlier.reshape(K * R, DE), pair_weight).astype(jnp.bfloat16).reshape(1, K * R, 2 * D)
        groups = jnp.concatenate([before, own_pairs], axis=0)
        hidden_f = block_rows.astype(jnp.float32)
        inv_rms = lax.rsqrt(lax.optimization_barrier(jnp.mean(hidden_f * hidden_f, axis=-1, keepdims=True)) + EPS)
        normed = (hidden_f * inv_rms * dec_gain).astype(jnp.bfloat16)
        queries = matmul(normed, cca_query).astype(jnp.bfloat16)
        padded = jnp.concatenate([jnp.zeros((1, D), jnp.bfloat16), queries, jnp.zeros((C - 1, D), jnp.bfloat16)], axis=0).reshape(CH_DEV + 1, C, D)
        context = attend(padded, groups)[1:TOK_DEV + 1]
        position = (column_index * TOK_DEV + jnp.arange(TOK_DEV, dtype=jnp.int32) + C) % SEQ_LEN
        context = jnp.where((position >= C - 1)[:, None], context, jnp.zeros_like(context))
        return (hidden_f + matmul(context, cca_out)).astype(jnp.bfloat16)
    mixed = lax.map(one_column, (blocks, groups_all, id_blocks, earlier_all, jnp.arange(COLUMNS, dtype=jnp.int32)))
    return (mixed.reshape(TOKENS, D), d_input.reshape(neighbours.shape), grads[0], grads[1], grads[2], grads[3])
```

```python
import jax
import jax.numpy as jnp
from jax import lax
from jax.sharding import PartitionSpec as P

HD = 128
DE = 896
EHEADS = 14
EHD = 64
C = 64
R = 128
K = 2
SEQ_LEN = 2048


EPS = 1e-06


def shifted(value, axis, steps):
    count = lax.axis_size(axis)
    initial, last = (max(0, -steps), min(count, count - steps))
    return lax.ppermute(value, axis, [(source, source + steps) for source in range(initial, last)])


def batched(pattern, former, latter):
    return jnp.einsum(pattern, former, latter, preferred_element_type=jnp.float32)


def matmul(former, latter):
    return jnp.dot(former, latter, preferred_element_type=jnp.float32)


def inner_rows(former, latter):
    return lax.dot_general(
        former, latter, (((0,), (0,)), ((), ())), preferred_element_type=jnp.float32
    )


def outer_cols(former, latter):
    return lax.dot_general(
        former, latter, (((1,), (1,)), ((), ())), preferred_element_type=jnp.float32
    )


def encode(rows_in, gain_vec, matrices, pieces):
    w_query, w_key, w_value, w_output = matrices
    x_float = rows_in.astype(jnp.float32)
    inv_rms = lax.rsqrt(jnp.mean(x_float * x_float, axis=-1, keepdims=True) + EPS)
    normed = (x_float * inv_rms * gain_vec).astype(jnp.bfloat16)
    layout = (pieces, R, EHEADS, EHD)
    queries = matmul(normed, w_query).astype(jnp.bfloat16).reshape(layout)
    keys_all = matmul(normed, w_key).astype(jnp.bfloat16).reshape(layout)
    values_all = matmul(normed, w_value).astype(jnp.bfloat16).reshape(layout)
    scores = batched("nqhd,nkhd->nhqk", queries, keys_all) * EHD ** (-0.5)
    soft_max = jax.nn.softmax(scores, axis=-1)
    soft_low = soft_max.astype(jnp.bfloat16)
    context = (
        batched("nhqk,nkhd->nqhd", soft_low, values_all)
        .astype(jnp.bfloat16)
        .reshape(pieces * R, DE)
    )
    encoded = (x_float + matmul(context, w_output)).astype(jnp.bfloat16)
    return (
        encoded,
        (x_float, inv_rms, normed, queries, keys_all, values_all, soft_max, soft_low, context),
    )


def encode_backward(cotangent, saved, matrices, gain_vec, pieces):
    w_query, w_key, w_value, w_output = matrices
    x_float, inv_rms, normed, queries, keys_all, values_all, soft_max, soft_low, context = saved
    layout = (pieces, R, EHEADS, EHD)
    grad_output = inner_rows(context, cotangent)
    d_context = outer_cols(cotangent, w_output).astype(jnp.bfloat16).reshape(layout)
    d_soft = batched("nqhd,nkhd->nhqk", d_context, values_all)
    d_values = (
        batched("nhqk,nqhd->nkhd", soft_low, d_context).astype(jnp.bfloat16).reshape(pieces * R, DE)
    )
    d_scores = (
        soft_max * (d_soft - jnp.sum(d_soft * soft_max, axis=-1, keepdims=True)) * EHD ** (-0.5)
    ).astype(jnp.bfloat16)
    d_queries = (
        batched("nhqk,nkhd->nqhd", d_scores, keys_all).astype(jnp.bfloat16).reshape(pieces * R, DE)
    )
    d_keys = (
        batched("nhqk,nqhd->nkhd", d_scores, queries).astype(jnp.bfloat16).reshape(pieces * R, DE)
    )
    grad_query = inner_rows(normed, d_queries)
    grad_key = inner_rows(normed, d_keys)
    grad_value = inner_rows(normed, d_values)
    d_normed = (
        outer_cols(d_queries, w_query) + outer_cols(d_keys, w_key) + outer_cols(d_values, w_value)
    )
    scaled = d_normed * gain_vec
    d_rows = inv_rms * scaled - x_float * inv_rms**3 * jnp.mean(
        x_float * scaled, axis=-1, keepdims=True
    )
    d_input = (cotangent.astype(jnp.float32) + d_rows).astype(jnp.bfloat16)
    return (d_input, (grad_query, grad_key, grad_value, grad_output))


def swap(value, axis, distance):
    count = lax.axis_size(axis)
    return lax.ppermute(value, axis, [(i, i ^ distance) for i in range(count)])


def ordered(flag, mine, other, axis):
    low = jnp.where(flag == 0, mine, other)
    high = jnp.where(flag == 0, other, mine)
    return jnp.concatenate([low, high], axis=axis)


def gather_rows(blocks, core, chip, pair):
    half = blocks.shape[1] // 2
    sibling = swap(blocks, "enc", 1)
    part = lax.dynamic_slice_in_dim(blocks, pair * half, half, 1)
    across = swap(part, "enc", 2)
    beside = swap(across, "seq", 1)
    far = ordered(pair, across, beside, 1)
    far_sibling = swap(far, "enc", 1)
    near = ordered(core, blocks, sibling, 1)
    away = ordered(core, far, far_sibling, 1)
    return ordered(chip, near, away, 1)


def pick(value, index, axis):
    return lax.dynamic_index_in_dim(value, index, axis, keepdims=False)


def halve(value, index, axis, mesh_axis, distance):
    sent = swap(pick(value, 1 - index, axis), mesh_axis, distance)
    kept = pick(value, index, axis)
    return (kept.astype(jnp.float32) + sent.astype(jnp.float32)).astype(jnp.bfloat16)


def attend(grouped, pairs):
    group_count, span_rows, width_here = grouped.shape
    heads_here = width_here // HD
    key_rows = pairs.shape[1]
    split_q = grouped.reshape(group_count, span_rows, heads_here, HD)
    split_k = pairs[..., :width_here].reshape(group_count, key_rows, heads_here, HD)
    split_v = pairs[..., width_here:].reshape(group_count, key_rows, heads_here, HD)
    scores = batched("gqhd,gkhd->ghqk", split_q, split_k) * HD ** (-0.5)
    soft_max = jax.nn.softmax(scores, axis=-1)
    soft_low = soft_max.astype(jnp.bfloat16)
    return (
        batched("ghqk,gkhd->gqhd", soft_low, split_v)
        .astype(jnp.bfloat16)
        .reshape(group_count * span_rows, width_here)
    )


def on_device(
    hidden,
    dec_gain,
    cca_query,
    cca_key,
    cca_value,
    cca_out,
    neighbours,
    enc_gain,
    enc_query,
    enc_key,
    enc_value,
    enc_output,
    enc_cotangent,
    neighbour_ids,
):
    enc_count, seq_count = lax.axis_size("enc"), lax.axis_size("seq")
    enc_at, seq_at = lax.axis_index("enc"), lax.axis_index("seq")
    core, chip, pair, line = enc_at % 2, enc_at // 2, seq_at % 2, seq_at // 2
    lines = seq_count // 2
    first = gather_rows(jnp.stack([enc_query, enc_key]), core, chip, pair)
    second = gather_rows(jnp.stack([enc_value, enc_output]), core, chip, pair)
    matrices = (first[0], first[1], second[0], second[1])
    local_count = neighbours.shape[1]
    encoded, saved = encode(
        neighbours.reshape(local_count * R, DE), enc_gain, matrices, local_count
    )
    d_input, partials = encode_backward(
        enc_cotangent.reshape(local_count * R, DE), saved, matrices, enc_gain, local_count
    )
    own_rows = DE // (enc_count * seq_count)

    def split(grad):
        return grad.astype(jnp.bfloat16).reshape(2, 2, lines, 2, own_rows, DE)

    def reduce_pair(first_grad, second_grad, chip_first):
        both = jnp.stack([split(first_grad), split(second_grad)], axis=4)
        both = both.reshape(2, 2, lines, 2, 2 * own_rows, DE)
        held = halve(both, core, 1, "enc", 1)
        if chip_first:
            held = halve(held, chip, 0, "enc", 2)
            return halve(held, pair, 1, "seq", 1)
        held = halve(held, pair, 2, "seq", 1)
        return halve(held, chip, 0, "enc", 2)

    held = jnp.concatenate(
        [reduce_pair(partials[2], partials[3], True), reduce_pair(partials[0], partials[1], False)],
        axis=1,
    )
    total = pick(held, line, 0).astype(jnp.float32)
    for step in range(1, lines):
        block = pick(held, (line + step) % lines, 0)
        moved = [(i, (i + 2 * step) % seq_count) for i in range(seq_count)]
        total = total + lax.ppermute(block, "seq", moved).astype(jnp.float32)
    pool_total = local_count * enc_count * seq_count
    total = (total / pool_total).reshape(4, own_rows, DE)
    grads = (total[2], total[3], total[0], total[1])

    head_width = cca_key.shape[1]
    rows = local_count * R
    sibling = swap(encoded, "enc", 1)
    across = swap(encoded, "enc", 2)
    across_sibling = swap(across, "enc", 1)
    pool = jnp.stack([encoded, sibling, across, across_sibling]).reshape(
        enc_count * local_count, R, DE
    )
    owner = neighbour_ids // local_count
    place = (owner ^ enc_at) * local_count + neighbour_ids % local_count
    stretch_count = neighbour_ids.shape[0]
    own_rows_enc = jnp.take(pool, place, axis=0).reshape(stretch_count, K * R, DE)
    earlier_rows = shifted(own_rows_enc[stretch_count - 1], "seq", 1)
    weights = jnp.concatenate([cca_key, cca_value], axis=1)
    own_pairs = (
        matmul(own_rows_enc.reshape(stretch_count * K * R, DE), weights)
        .astype(jnp.bfloat16)
        .reshape(stretch_count, K * R, 2 * head_width)
    )
    earlier = matmul(earlier_rows, weights).astype(jnp.bfloat16)
    hidden_f = hidden.astype(jnp.float32)
    inv_rms = lax.rsqrt(jnp.mean(hidden_f * hidden_f, axis=-1, keepdims=True) + EPS)
    normed = (hidden_f * inv_rms * dec_gain).astype(jnp.bfloat16)
    queries = matmul(normed, cca_query).astype(jnp.bfloat16)
    token_count = hidden.shape[0]
    groups = jnp.concatenate([earlier[None], own_pairs], axis=0)
    padded = jnp.concatenate(
        [
            jnp.zeros((1, head_width), jnp.bfloat16),
            queries,
            jnp.zeros((C - 1, head_width), jnp.bfloat16),
        ],
        axis=0,
    ).reshape(stretch_count + 1, C, head_width)
    context = attend(padded, groups)[1 : token_count + 1]
    position = (
        seq_at * token_count + jnp.arange(token_count, dtype=jnp.int32) + C
    ) % SEQ_LEN
    context = jnp.where((position >= C - 1)[:, None], context, jnp.zeros_like(context))
    wide = cca_out.shape[1] // 2
    slice_width = wide // 2

    def out_half(which):
        columns = lax.dynamic_slice_in_dim(cca_out, which * wide, wide, 1)
        return matmul(context, columns).astype(jnp.bfloat16).reshape(token_count, 2, slice_width)

    far_part = out_half(1 - chip)
    far_sum = halve(far_part, core, 1, "enc", 1)
    landed = swap(far_sum, "enc", 2)
    near_part = out_half(chip)
    near_sent = swap(pick(near_part, 1 - core, 1), "enc", 1)
    branch = (
        pick(near_part, core, 1).astype(jnp.float32)
        + near_sent.astype(jnp.float32)
        + landed.astype(jnp.float32)
    )
    residual = lax.dynamic_slice_in_dim(hidden, enc_at * slice_width, slice_width, 1)
    mixed = (residual.astype(jnp.float32) + branch).astype(jnp.bfloat16)
    return (mixed, d_input.reshape(neighbours.shape), grads[0], grads[1], grads[2], grads[3])


def solution(mesh):
    return jax.shard_map(
        on_device,
        mesh=mesh,
        in_specs=(
            P("seq", None),
            P(),
            P(None, "enc"),
            P(None, "enc"),
            P(None, "enc"),
            P("enc", None),
            P("seq", "enc", None, None),
            P(),
            P("enc", None),
            P("enc", None),
            P("enc", None),
            P("enc", None),
            P("seq", "enc", None, None),
            P("seq", None),
        ),
        out_specs=(
            P("seq", "enc"),
            P("seq", "enc", None, None),
            P(("enc", "seq"), None),
            P(("enc", "seq"), None),
            P(("enc", "seq"), None),
            P(("enc", "seq"), None),
        ),
        check_vma=False,
    )
```

```python
import jax
import jax.numpy as jnp
from jax import lax
from jax.experimental import pallas as pl
from jax.experimental.pallas import tpu as pltpu
from jax.sharding import PartitionSpec as P

HD = 128
DE = 896
EHEADS = 14
EHD = 64
C = 64
R = 128
K = 2
SEQ_LEN = 2048


EPS = 1e-06


def shifted(value, axis, steps):
    count = lax.axis_size(axis)
    initial, last = (max(0, -steps), min(count, count - steps))
    return lax.ppermute(value, axis, [(source, source + steps) for source in range(initial, last)])


def matmul(former, latter):
    return jnp.dot(former, latter, preferred_element_type=jnp.float32)


def inner_rows(former, latter):
    return lax.dot_general(
        former, latter, (((0,), (0,)), ((), ())), preferred_element_type=jnp.float32
    )


def outer_cols(former, latter):
    return lax.dot_general(
        former, latter, (((1,), (1,)), ((), ())), preferred_element_type=jnp.float32
    )


def two_heads(block):
    low = lax.broadcasted_iota(jnp.int32, block.shape, 1) < EHD
    zero = jnp.zeros_like(block)
    return jnp.concatenate([jnp.where(low, block, zero), jnp.where(low, zero, block)], axis=0)


def join_heads(stacked):
    half = stacked.shape[0] // 2
    low = lax.broadcasted_iota(jnp.int32, (half, stacked.shape[1]), 1) < EHD
    return jnp.where(low, stacked[:half], stacked[half:])


def softmax(scores):
    powers = jnp.exp(scores - jnp.max(scores, axis=-1, keepdims=True))
    return powers / jnp.sum(powers, axis=-1, keepdims=True)


def units(rows):
    pairs = EHEADS * EHD // 128
    return [
        (n * pairs + h, slice(n * R, (n + 1) * R), slice(h * 128, (h + 1) * 128))
        for n in range(rows // R)
        for h in range(pairs)
    ]


def forward_kernel(
    x_ref, gain_ref, qk_ref, vo_ref, enc_ref, normed_ref, q_ref, k_ref, v_ref, p_ref, ctx_ref
):
    x = x_ref[...].astype(jnp.float32)
    inv_rms = lax.rsqrt(jnp.mean(x * x, axis=-1, keepdims=True) + EPS)
    normed_ref[...] = (x * inv_rms * gain_ref[...]).astype(jnp.bfloat16)
    normed = normed_ref[...]
    q_ref[...] = matmul(normed, qk_ref[0]).astype(jnp.bfloat16)
    k_ref[...] = matmul(normed, qk_ref[1]).astype(jnp.bfloat16)
    v_ref[...] = matmul(normed, vo_ref[0]).astype(jnp.bfloat16)
    for at, rows, lanes in units(x_ref.shape[0]):
        scores = outer_cols(two_heads(q_ref[rows, lanes]), k_ref[rows, lanes]) * EHD ** (-0.5)
        weight = softmax(scores)
        p_ref[at] = weight
        ctx_ref[rows, lanes] = join_heads(
            matmul(weight.astype(jnp.bfloat16), v_ref[rows, lanes])
        ).astype(jnp.bfloat16)
    enc_ref[...] = (
        x_ref[...].astype(jnp.float32) + matmul(ctx_ref[...], vo_ref[1])
    ).astype(jnp.bfloat16)


def backward_kernel(
    x_ref,
    gain_ref,
    cot_ref,
    qk_ref,
    vo_ref,
    normed_ref,
    q_ref,
    k_ref,
    v_ref,
    p_ref,
    ctx_ref,
    order_a_ref,
    order_b_ref,
    dx_ref,
    a_keep,
    a_send,
    b_keep,
    b_send,
    dctx,
    dq,
    dk,
    dv,
):
    half = a_keep.shape[1]

    def emit(which, keep, send, former, latter):
        keep[which] = matmul(former[:half], latter).astype(jnp.bfloat16)
        send[which] = matmul(former[half:], latter).astype(jnp.bfloat16)

    dctx[...] = outer_cols(cot_ref[...], vo_ref[1]).astype(jnp.bfloat16)
    for at, rows, lanes in units(x_ref.shape[0]):
        d_context = two_heads(dctx[rows, lanes])
        weight = p_ref[at]
        d_p = outer_cols(d_context, v_ref[rows, lanes])
        dv[rows, lanes] = inner_rows(weight.astype(jnp.bfloat16), d_context).astype(jnp.bfloat16)
        d_s = (
            weight
            * (d_p - jnp.sum(d_p * weight, axis=-1, keepdims=True))
            * EHD ** (-0.5)
        ).astype(jnp.bfloat16)
        dq[rows, lanes] = join_heads(matmul(d_s, k_ref[rows, lanes])).astype(jnp.bfloat16)
        dk[rows, lanes] = inner_rows(d_s, two_heads(q_ref[rows, lanes])).astype(jnp.bfloat16)
    rows_a = outer_cols(order_a_ref[...], normed_ref[...]).astype(jnp.bfloat16)
    emit(0, a_keep, a_send, rows_a, dv[...])
    rows_o = outer_cols(order_a_ref[...], ctx_ref[...]).astype(jnp.bfloat16)
    emit(1, a_keep, a_send, rows_o, cot_ref[...])
    rows_b = outer_cols(order_b_ref[...], normed_ref[...]).astype(jnp.bfloat16)
    emit(0, b_keep, b_send, rows_b, dq[...])
    emit(1, b_keep, b_send, rows_b, dk[...])
    d_normed = (
        outer_cols(dq[...], qk_ref[0])
        + outer_cols(dk[...], qk_ref[1])
        + outer_cols(dv[...], vo_ref[0])
    )
    scaled = d_normed * gain_ref[...]
    x = x_ref[...].astype(jnp.float32)
    inv_rms = lax.rsqrt(jnp.mean(x * x, axis=-1, keepdims=True) + EPS)
    d_rows = inv_rms * scaled - x * inv_rms**3 * jnp.mean(x * scaled, axis=-1, keepdims=True)
    dx_ref[...] = (cot_ref[...].astype(jnp.float32) + d_rows).astype(jnp.bfloat16)


def decode_kernel(place_ref, q_ref, wk_ref, wv_ref, *refs):
    pieces, (ctx_ref, kv) = refs[:-2], refs[-2:]
    weights = jnp.concatenate([wk_ref[...], wv_ref[...]], axis=1)
    rows = pieces[0].shape[0]
    for at, piece in enumerate(pieces):
        kv[at * rows : (at + 1) * rows, :] = matmul(piece[...], weights).astype(jnp.bfloat16)
    for group in range(q_ref.shape[0] // C):
        span = slice(group * C, (group + 1) * C)
        query = q_ref[span, :]
        blocks = [kv[pl.ds(pl.multiple_of(place_ref[group, i] * R, R), R), :] for i in range(K)]
        scores = jnp.concatenate([outer_cols(query, b[:, :HD]) for b in blocks], axis=1)
        weight = softmax(scores * HD ** (-0.5)).astype(jnp.bfloat16)
        total = matmul(weight[:, :R], blocks[0][:, HD:])
        for i in range(1, K):
            total = total + matmul(weight[:, i * R : (i + 1) * R], blocks[i][:, HD:])
        ctx_ref[span, :] = total.astype(jnp.bfloat16)


LIMIT = 52 * 1024 * 1024


def decode(place, queries, key_weight, value_weight, pieces):
    count, width = queries.shape
    whole = [pl.BlockSpec(piece.shape, lambda h: (0, 0)) for piece in pieces]
    rows = sum(piece.shape[0] for piece in pieces)
    column = lambda h: (0, h)
    flops = 2 * rows * DE * 2 * width + 4 * count * K * R * width
    return pl.pallas_call(
        decode_kernel,
        grid=(width // HD,),
        out_shape=jax.ShapeDtypeStruct((count, width), jnp.bfloat16),
        in_specs=[
            pl.BlockSpec(memory_space=pltpu.SMEM),
            pl.BlockSpec((count, HD), column),
            pl.BlockSpec((DE, HD), column),
            pl.BlockSpec((DE, HD), column),
        ]
        + whole,
        out_specs=pl.BlockSpec((count, HD), column),
        scratch_shapes=[pltpu.VMEM((rows, 2 * HD), jnp.bfloat16)],
        compiler_params=pltpu.CompilerParams(vmem_limit_bytes=LIMIT),
        cost_estimate=pl.CostEstimate(
            flops=2 * flops, bytes_accessed=rows * DE * 2 + 4 * DE * width, transcendentals=0
        ),
    )(place, queries, key_weight, value_weight, *pieces)


def one_call(kernel, outs, scratch, args, flops):
    vmem = pl.BlockSpec(memory_space=pltpu.VMEM)
    size = sum(a.size * a.dtype.itemsize for a in (*args, *outs))
    return pl.pallas_call(
        kernel,
        out_shape=outs,
        in_specs=[vmem] * len(args),
        out_specs=[vmem] * len(outs),
        scratch_shapes=scratch,
        compiler_params=pltpu.CompilerParams(vmem_limit_bytes=LIMIT),
        cost_estimate=pl.CostEstimate(flops=flops, bytes_accessed=size, transcendentals=0),
    )(*args)


def swap(value, axis, distance):
    count = lax.axis_size(axis)
    return lax.ppermute(value, axis, [(i, i ^ distance) for i in range(count)])


def ordered(flag, mine, other, axis):
    low = jnp.where(flag == 0, mine, other)
    high = jnp.where(flag == 0, other, mine)
    return jnp.concatenate([low, high], axis=axis)


def gather_rows(blocks, core, chip, pair):
    half = blocks.shape[1] // 2
    sibling = swap(blocks, "enc", 1)
    part = lax.dynamic_slice_in_dim(blocks, pair * half, half, 1)
    across = swap(part, "enc", 2)
    beside = swap(across, "seq", 1)
    far = ordered(pair, across, beside, 1)
    far_sibling = swap(far, "enc", 1)
    near = ordered(core, blocks, sibling, 1)
    away = ordered(core, far, far_sibling, 1)
    return ordered(chip, near, away, 1)


def pick(value, index, axis):
    return lax.dynamic_index_in_dim(value, index, axis, keepdims=False)


def on_device(
    hidden,
    dec_gain,
    cca_query,
    cca_key,
    cca_value,
    cca_out,
    neighbours,
    enc_gain,
    enc_query,
    enc_key,
    enc_value,
    enc_output,
    enc_cotangent,
    neighbour_ids,
):
    enc_count, seq_count = lax.axis_size("enc"), lax.axis_size("seq")
    enc_at, seq_at = lax.axis_index("enc"), lax.axis_index("seq")
    core, chip, pair, line = enc_at % 2, enc_at // 2, seq_at % 2, seq_at // 2
    lines = seq_count // 2
    first = gather_rows(jnp.stack([enc_query, enc_key]), core, chip, pair)
    second = gather_rows(jnp.stack([enc_value, enc_output]), core, chip, pair)
    local_count = neighbours.shape[1]
    rows = local_count * R
    x_rows = neighbours.reshape(rows, DE)
    cotangent = enc_cotangent.reshape(rows, DE)
    gain = enc_gain.reshape(1, DE)
    low = jax.ShapeDtypeStruct((rows, DE), jnp.bfloat16)
    soft = jax.ShapeDtypeStruct((rows // R * (DE // 128), 2 * R, R), jnp.float32)
    encoded, normed_rows, enc_q, enc_k, enc_v, enc_p, enc_ctx = one_call(
        forward_kernel,
        [low, low, low, low, low, soft, low],
        [],
        (x_rows, gain, first, second),
        12 * rows * DE * DE,
    )
    own_rows = DE // (enc_count * seq_count)
    target = jnp.arange(DE, dtype=jnp.int32)
    inner, block = target % own_rows, target // own_rows
    ahead = (line + block % lines) % lines
    low_bit, mid_bit, top_bit = (
        block // lines % 2,
        block // lines // 2 % 2,
        block // lines // 4,
    )

    def order(chip_bit, pair_bit):
        device = ((chip ^ chip_bit) * 2 + (core ^ top_bit)) * seq_count + ahead * 2 + (
            pair ^ pair_bit
        )
        return (target[None, :] == (device * own_rows + inner)[:, None]).astype(jnp.bfloat16)

    part = jax.ShapeDtypeStruct((2, DE // 2, DE), jnp.bfloat16)
    space = [pltpu.VMEM((rows, DE), jnp.bfloat16)] * 4
    d_input, a_keep, a_send, b_keep, b_send = one_call(
        backward_kernel,
        [low, part, part, part, part],
        space,
        (
            x_rows,
            gain,
            cotangent,
            first,
            second,
            normed_rows,
            enc_q,
            enc_k,
            enc_v,
            enc_p,
            enc_ctx,
            order(mid_bit, low_bit),
            order(low_bit, mid_bit),
        ),
        28 * rows * DE * DE,
    )

    def added(former, latter):
        return (former.astype(jnp.float32) + latter.astype(jnp.float32)).astype(jnp.bfloat16)

    def reduce_pair(keep, send, routes):
        came = swap(send, "enc", 1)
        for axis, distance in routes:
            half = keep.shape[1] // 2
            send = added(keep[:, half:], came[:, half:])
            keep = added(keep[:, :half], came[:, :half])
            came = swap(send, axis, distance)
        return added(keep, came)

    held = jnp.concatenate(
        [
            reduce_pair(a_keep, a_send, (("enc", 2), ("seq", 1))),
            reduce_pair(b_keep, b_send, (("seq", 1), ("enc", 2))),
        ],
        axis=0,
    ).reshape(4, lines, own_rows, DE)
    total = held[:, 0].astype(jnp.float32)
    for step in range(1, lines):
        moved = [(i, (i + 2 * step) % seq_count) for i in range(seq_count)]
        total = total + lax.ppermute(held[:, step], "seq", moved).astype(jnp.float32)
    total = total / (local_count * enc_count * seq_count)
    grads = (total[2], total[3], total[0], total[1])

    head_width = cca_key.shape[1]
    sibling = swap(encoded, "enc", 1)
    across = swap(encoded, "enc", 2)
    across_sibling = swap(across, "enc", 1)
    pieces = (encoded, sibling, across, across_sibling)
    owner = neighbour_ids // local_count
    place = (owner ^ enc_at) * local_count + neighbour_ids % local_count
    stretch_count = neighbour_ids.shape[0]
    tokens = [piece.reshape(local_count, R, DE) for piece in pieces]

    def chosen(at):
        value = tokens[0][0]
        for i in range(1, enc_count * local_count):
            value = jnp.where(at == i, tokens[i // local_count][i % local_count], value)
        return value

    last = jnp.concatenate([chosen(place[stretch_count - 1, i]) for i in range(K)], axis=0)
    earlier_rows = shifted(last, "seq", 1)
    hidden_f = hidden.astype(jnp.float32)
    inv_rms = lax.rsqrt(jnp.mean(hidden_f * hidden_f, axis=-1, keepdims=True) + EPS)
    normed = (hidden_f * inv_rms * dec_gain).astype(jnp.bfloat16)
    token_count, model_width = hidden.shape
    padded = jnp.concatenate(
        [
            jnp.zeros((1, model_width), jnp.bfloat16),
            normed,
            jnp.zeros((C - 1, model_width), jnp.bfloat16),
        ],
        axis=0,
    )
    queries = matmul(padded, cca_query).astype(jnp.bfloat16)
    own_context = decode(place, queries[C:], cca_key, cca_value, pieces)
    in_order = jnp.arange(K, dtype=jnp.int32).reshape(1, K)
    early_context = decode(in_order, queries[:C], cca_key, cca_value, (earlier_rows,))
    context = jnp.concatenate([early_context, own_context], axis=0)[1 : token_count + 1]
    position = (
        seq_at * token_count + jnp.arange(token_count, dtype=jnp.int32) + C
    ) % SEQ_LEN
    context = jnp.where((position >= C - 1)[:, None], context, jnp.zeros_like(context))
    wide = cca_out.shape[1] // 2
    slice_width = wide // 2

    def out_half(which):
        columns = lax.dynamic_slice_in_dim(cca_out, which * wide, wide, 1)
        return matmul(context, columns).astype(jnp.bfloat16).reshape(token_count, 2, slice_width)

    far_part = out_half(1 - chip)
    far_sum = added(
        pick(far_part, core, 1), swap(pick(far_part, 1 - core, 1), "enc", 1)
    )
    landed = swap(far_sum, "enc", 2)
    near_part = out_half(chip)
    near_sent = swap(pick(near_part, 1 - core, 1), "enc", 1)
    branch = (
        pick(near_part, core, 1).astype(jnp.float32)
        + near_sent.astype(jnp.float32)
        + landed.astype(jnp.float32)
    )
    residual = lax.dynamic_slice_in_dim(hidden, enc_at * slice_width, slice_width, 1)
    mixed = (residual.astype(jnp.float32) + branch).astype(jnp.bfloat16)
    return (mixed, d_input.reshape(neighbours.shape), grads[0], grads[1], grads[2], grads[3])


def solution(mesh):
    return jax.shard_map(
        on_device,
        mesh=mesh,
        in_specs=(
            P("seq", None),
            P(),
            P(None, "enc"),
            P(None, "enc"),
            P(None, "enc"),
            P("enc", None),
            P("seq", "enc", None, None),
            P(),
            P("enc", None),
            P("enc", None),
            P("enc", None),
            P("enc", None),
            P("seq", "enc", None, None),
            P("seq", None),
        ),
        out_specs=(
            P("seq", "enc"),
            P("seq", "enc", None, None),
            P(("enc", "seq"), None),
            P(("enc", "seq"), None),
            P(("enc", "seq"), None),
            P(("enc", "seq"), None),
        ),
        check_vma=False,
    )
```

```python
import jax
import jax.numpy as jnp
from jax import lax
from jax.experimental import pallas as pl
from jax.experimental.pallas import tpu as pltpu
from jax.sharding import PartitionSpec as P

HD = 128
DE = 896
EHEADS = 14
EHD = 64
C = 64
R = 128
K = 2
SEQ_LEN = 2048


EPS = 1e-06


def shifted(value, axis, steps):
    count = lax.axis_size(axis)
    initial, last = (max(0, -steps), min(count, count - steps))
    return lax.ppermute(value, axis, [(source, source + steps) for source in range(initial, last)])


def matmul(former, latter):
    return jnp.dot(former, latter, preferred_element_type=jnp.float32)


def inner_rows(former, latter):
    return lax.dot_general(
        former, latter, (((0,), (0,)), ((), ())), preferred_element_type=jnp.float32
    )


def outer_cols(former, latter):
    return lax.dot_general(
        former, latter, (((1,), (1,)), ((), ())), preferred_element_type=jnp.float32
    )


def two_heads(block):
    low = lax.broadcasted_iota(jnp.int32, block.shape, 1) < EHD
    zero = jnp.zeros_like(block)
    return jnp.concatenate([jnp.where(low, block, zero), jnp.where(low, zero, block)], axis=0)


def join_heads(stacked):
    half = stacked.shape[0] // 2
    low = lax.broadcasted_iota(jnp.int32, (half, stacked.shape[1]), 1) < EHD
    return jnp.where(low, stacked[:half], stacked[half:])


def softmax(scores):
    powers = jnp.exp(scores - jnp.max(scores, axis=-1, keepdims=True))
    return powers / jnp.sum(powers, axis=-1, keepdims=True)


def units(rows):
    pairs = EHEADS * EHD // 128
    return [
        (n * pairs + h, slice(n * R, (n + 1) * R), slice(h * 128, (h + 1) * 128))
        for n in range(rows // R)
        for h in range(pairs)
    ]


def forward_kernel(
    x_ref, gain_ref, qk_ref, vo_ref, enc_ref, normed_ref, q_ref, k_ref, v_ref, p_ref, ctx_ref
):
    x = x_ref[...].astype(jnp.float32)
    inv_rms = lax.rsqrt(jnp.mean(x * x, axis=-1, keepdims=True) + EPS)
    normed_ref[...] = (x * inv_rms * gain_ref[...]).astype(jnp.bfloat16)
    normed = normed_ref[...]
    q_ref[...] = matmul(normed, qk_ref[0]).astype(jnp.bfloat16)
    k_ref[...] = matmul(normed, qk_ref[1]).astype(jnp.bfloat16)
    v_ref[...] = matmul(normed, vo_ref[0]).astype(jnp.bfloat16)
    for at, rows, lanes in units(x_ref.shape[0]):
        scores = outer_cols(two_heads(q_ref[rows, lanes]), k_ref[rows, lanes]) * EHD ** (-0.5)
        weight = softmax(scores)
        p_ref[at] = weight
        ctx_ref[rows, lanes] = join_heads(
            matmul(weight.astype(jnp.bfloat16), v_ref[rows, lanes])
        ).astype(jnp.bfloat16)
    enc_ref[...] = (
        x_ref[...].astype(jnp.float32) + matmul(ctx_ref[...], vo_ref[1])
    ).astype(jnp.bfloat16)


def backward_kernel(
    x_ref,
    gain_ref,
    cot_ref,
    qk_ref,
    vo_ref,
    normed_ref,
    q_ref,
    k_ref,
    v_ref,
    p_ref,
    ctx_ref,
    order_a_ref,
    order_b_ref,
    dx_ref,
    a_keep,
    a_send,
    b_keep,
    b_send,
    dctx,
    dq,
    dk,
    dv,
):
    half = a_keep.shape[1]

    def emit(which, keep, send, former, latter):
        keep[which] = matmul(former[:half], latter).astype(jnp.bfloat16)
        send[which] = matmul(former[half:], latter).astype(jnp.bfloat16)

    dctx[...] = outer_cols(cot_ref[...], vo_ref[1]).astype(jnp.bfloat16)
    for at, rows, lanes in units(x_ref.shape[0]):
        d_context = two_heads(dctx[rows, lanes])
        weight = p_ref[at]
        d_p = outer_cols(d_context, v_ref[rows, lanes])
        dv[rows, lanes] = inner_rows(weight.astype(jnp.bfloat16), d_context).astype(jnp.bfloat16)
        d_s = (
            weight
            * (d_p - jnp.sum(d_p * weight, axis=-1, keepdims=True))
            * EHD ** (-0.5)
        ).astype(jnp.bfloat16)
        dq[rows, lanes] = join_heads(matmul(d_s, k_ref[rows, lanes])).astype(jnp.bfloat16)
        dk[rows, lanes] = inner_rows(d_s, two_heads(q_ref[rows, lanes])).astype(jnp.bfloat16)
    rows_a = outer_cols(order_a_ref[...], normed_ref[...]).astype(jnp.bfloat16)
    emit(0, a_keep, a_send, rows_a, dv[...])
    rows_o = outer_cols(order_a_ref[...], ctx_ref[...]).astype(jnp.bfloat16)
    emit(1, a_keep, a_send, rows_o, cot_ref[...])
    rows_b = outer_cols(order_b_ref[...], normed_ref[...]).astype(jnp.bfloat16)
    emit(0, b_keep, b_send, rows_b, dq[...])
    emit(1, b_keep, b_send, rows_b, dk[...])
    d_normed = (
        outer_cols(dq[...], qk_ref[0])
        + outer_cols(dk[...], qk_ref[1])
        + outer_cols(dv[...], vo_ref[0])
    )
    scaled = d_normed * gain_ref[...]
    x = x_ref[...].astype(jnp.float32)
    inv_rms = lax.rsqrt(jnp.mean(x * x, axis=-1, keepdims=True) + EPS)
    d_rows = inv_rms * scaled - x * inv_rms**3 * jnp.mean(x * scaled, axis=-1, keepdims=True)
    dx_ref[...] = (cot_ref[...].astype(jnp.float32) + d_rows).astype(jnp.bfloat16)


HEADS_STEP = 2


def decode_kernel(place_ref, q_ref, wk_ref, wv_ref, *refs):
    pieces, (ctx_ref, kv) = refs[:-2], refs[-2:]
    weights = jnp.concatenate([wk_ref[...], wv_ref[...]], axis=1)
    rows = pieces[0].shape[0]
    for at, piece in enumerate(pieces):
        kv[at * rows : (at + 1) * rows, :] = matmul(piece[...], weights).astype(jnp.bfloat16)
    groups = q_ref.shape[0] // C
    for head in range(HEADS_STEP):
        lanes = slice(head * HD, (head + 1) * HD)
        value_lanes = slice((HEADS_STEP + head) * HD, (HEADS_STEP + head + 1) * HD)
        scores, spots = [], []
        for group in range(groups):
            query = q_ref[group * C : (group + 1) * C, lanes]
            spot = [pl.ds(pl.multiple_of(place_ref[group, i] * R, R), R) for i in range(K)]
            scores.append(
                jnp.concatenate([outer_cols(query, kv[rows, lanes]) for rows in spot], axis=1)
            )
            spots.append(spot)
        weight = softmax(jnp.concatenate(scores, axis=0) * HD ** (-0.5)).astype(jnp.bfloat16)
        for group in range(groups):
            part = weight[group * C : (group + 1) * C]
            total = matmul(part[:, :R], kv[spots[group][0], value_lanes])
            for i in range(1, K):
                total = total + matmul(
                    part[:, i * R : (i + 1) * R], kv[spots[group][i], value_lanes]
                )
            ctx_ref[group * C : (group + 1) * C, lanes] = total.astype(jnp.bfloat16)


LIMIT = 52 * 1024 * 1024


def decode(place, queries, key_weight, value_weight, pieces):
    count, width = queries.shape
    whole = [pl.BlockSpec(piece.shape, lambda h: (0, 0)) for piece in pieces]
    rows = sum(piece.shape[0] for piece in pieces)
    column = lambda h: (0, h)
    flops = 2 * rows * DE * 2 * width + 4 * count * K * R * width
    return pl.pallas_call(
        decode_kernel,
        grid=(width // (HEADS_STEP * HD),),
        out_shape=jax.ShapeDtypeStruct((count, width), jnp.bfloat16),
        in_specs=[
            pl.BlockSpec(memory_space=pltpu.SMEM),
            pl.BlockSpec((count, HEADS_STEP * HD), column),
            pl.BlockSpec((DE, HEADS_STEP * HD), column),
            pl.BlockSpec((DE, HEADS_STEP * HD), column),
        ]
        + whole,
        out_specs=pl.BlockSpec((count, HEADS_STEP * HD), column),
        scratch_shapes=[pltpu.VMEM((rows, 2 * HEADS_STEP * HD), jnp.bfloat16)],
        compiler_params=pltpu.CompilerParams(vmem_limit_bytes=LIMIT),
        cost_estimate=pl.CostEstimate(
            flops=2 * flops, bytes_accessed=rows * DE * 2 + 4 * DE * width, transcendentals=0
        ),
    )(place, queries, key_weight, value_weight, *pieces)


def one_call(kernel, outs, scratch, args, flops):
    vmem = pl.BlockSpec(memory_space=pltpu.VMEM)
    size = sum(a.size * a.dtype.itemsize for a in (*args, *outs))
    return pl.pallas_call(
        kernel,
        out_shape=outs,
        in_specs=[vmem] * len(args),
        out_specs=[vmem] * len(outs),
        scratch_shapes=scratch,
        compiler_params=pltpu.CompilerParams(vmem_limit_bytes=LIMIT),
        cost_estimate=pl.CostEstimate(flops=flops, bytes_accessed=size, transcendentals=0),
    )(*args)


def swap(value, axis, distance):
    count = lax.axis_size(axis)
    return lax.ppermute(value, axis, [(i, i ^ distance) for i in range(count)])


def gather_kernel(q_ref, k_ref, v_ref, o_ref, qk_ref, vo_ref, local_sem, send_sem, recv_sem):
    enc_at, seq_at = lax.axis_index("enc"), lax.axis_index("seq")
    pair = seq_at % 2
    sibling = (enc_at + 1 - 2 * (enc_at % 2), seq_at)
    across = ((enc_at + 2) % 4, seq_at)
    beside = (enc_at, seq_at + 1 - 2 * pair)
    height = q_ref.shape[0]
    half = height // 2
    barrier = pltpu.get_barrier_semaphore()
    for other in (sibling, across, beside):
        pl.semaphore_signal(barrier, inc=1, device_id=other, device_id_type=pl.DeviceIdType.MESH)
    pl.semaphore_wait(barrier, 3)

    def place(which, start, count):
        out = (qk_ref, vo_ref)[which // 2]
        return out.at[which % 2, pl.ds(pl.multiple_of(start, 16), count)]

    def send(kind, which, source, target, other):
        copy = pltpu.make_async_remote_copy(
            src_ref=source,
            dst_ref=target,
            send_sem=send_sem.at[kind, which],
            recv_sem=recv_sem.at[kind, which],
            device_id=other,
            device_id_type=pl.DeviceIdType.MESH,
        )
        copy.start()
        return copy

    blocks = (q_ref, k_ref, v_ref, o_ref)
    far = ((enc_at + 2) % 4) * height
    mine = enc_at * height
    copies, crossing, beside_copies = [], [], []
    for which, block in enumerate(blocks):
        rows = pl.ds(pl.multiple_of(pair * half, 16), half)
        crossing.append(
            send(0, which, block.at[rows], place(which, mine + pair * half, half), across)
        )
    for which, block in enumerate(blocks):
        copies.append(send(1, which, block, place(which, mine, height), sibling))
    locals_ = []
    for which, block in enumerate(blocks):
        copy = pltpu.make_async_copy(block, place(which, mine, height), local_sem.at[which])
        copy.start()
        locals_.append(copy)
    for which in range(4):
        crossing[which].wait_recv()
        landed = place(which, far + pair * half, half)
        beside_copies.append(send(2, which, landed, landed, beside))
        copies.append(send(3, which, landed, landed, sibling))
    for which in range(4):
        beside_copies[which].wait_recv()
        landed = place(which, far + (1 - pair) * half, half)
        copies.append(send(4, which, landed, landed, sibling))
    for copy in crossing + beside_copies:
        copy.wait_send()
    for copy in copies:
        copy.wait()
    for copy in locals_:
        copy.wait()


def gather_weights(blocks, count):
    height, width = blocks[0].shape
    out = jax.ShapeDtypeStruct((2, count * height, width), blocks[0].dtype)
    anywhere = pl.BlockSpec(memory_space=pl.ANY)
    return pl.pallas_call(
        gather_kernel,
        out_shape=[out, out],
        in_specs=[anywhere] * 4,
        out_specs=[anywhere] * 2,
        scratch_shapes=[
            pltpu.SemaphoreType.DMA((4,)),
            pltpu.SemaphoreType.DMA((5, 4)),
            pltpu.SemaphoreType.DMA((5, 4)),
        ],
        compiler_params=pltpu.CompilerParams(
            collective_id=0, has_side_effects=True, vmem_limit_bytes=LIMIT
        ),
    )(*blocks)


def project_kernel(_, context_ref, weight_ref, out_ref):
    out_ref[...] = matmul(context_ref[...], weight_ref[...]).astype(jnp.bfloat16)


def project(context, weight, which, count):
    tokens, depth = context.shape
    width = weight.shape[1] // count
    steps = 4
    tile = width // steps
    return pl.pallas_call(
        project_kernel,
        out_shape=jax.ShapeDtypeStruct((tokens, width), jnp.bfloat16),
        grid_spec=pltpu.PrefetchScalarGridSpec(
            num_scalar_prefetch=1,
            grid=(steps,),
            in_specs=[
                pl.BlockSpec((tokens, depth), lambda i, at: (0, 0)),
                pl.BlockSpec((depth, tile), lambda i, at: (0, at[0] * steps + i)),
            ],
            out_specs=pl.BlockSpec((tokens, tile), lambda i, at: (0, i)),
        ),
        compiler_params=pltpu.CompilerParams(vmem_limit_bytes=LIMIT),
        cost_estimate=pl.CostEstimate(
            flops=2 * tokens * depth * width, bytes_accessed=2 * depth * width, transcendentals=0
        ),
    )(which.astype(jnp.int32).reshape(1), context, weight)


def on_device(
    hidden,
    dec_gain,
    cca_query,
    cca_key,
    cca_value,
    cca_out,
    neighbours,
    enc_gain,
    enc_query,
    enc_key,
    enc_value,
    enc_output,
    enc_cotangent,
    neighbour_ids,
):
    enc_count, seq_count = lax.axis_size("enc"), lax.axis_size("seq")
    enc_at, seq_at = lax.axis_index("enc"), lax.axis_index("seq")
    core, chip, pair, line = enc_at % 2, enc_at // 2, seq_at % 2, seq_at // 2
    lines = seq_count // 2
    first, second = gather_weights((enc_query, enc_key, enc_value, enc_output), enc_count)
    local_count = neighbours.shape[1]
    rows = local_count * R
    x_rows = neighbours.reshape(rows, DE)
    cotangent = enc_cotangent.reshape(rows, DE)
    gain = enc_gain.reshape(1, DE)
    low = jax.ShapeDtypeStruct((rows, DE), jnp.bfloat16)
    soft = jax.ShapeDtypeStruct((rows // R * (DE // 128), 2 * R, R), jnp.float32)
    encoded, normed_rows, enc_q, enc_k, enc_v, enc_p, enc_ctx = one_call(
        forward_kernel,
        [low, low, low, low, low, soft, low],
        [],
        (x_rows, gain, first, second),
        12 * rows * DE * DE,
    )
    own_rows = DE // (enc_count * seq_count)
    target = jnp.arange(DE, dtype=jnp.int32)
    inner, block = target % own_rows, target // own_rows
    ahead = (line + block % lines) % lines
    low_bit, mid_bit, top_bit = (
        block // lines % 2,
        block // lines // 2 % 2,
        block // lines // 4,
    )

    def order(chip_bit, pair_bit):
        device = ((chip ^ chip_bit) * 2 + (core ^ top_bit)) * seq_count + ahead * 2 + (
            pair ^ pair_bit
        )
        return (target[None, :] == (device * own_rows + inner)[:, None]).astype(jnp.bfloat16)

    part = jax.ShapeDtypeStruct((2, DE // 2, DE), jnp.bfloat16)
    space = [pltpu.VMEM((rows, DE), jnp.bfloat16)] * 4
    d_input, a_keep, a_send, b_keep, b_send = one_call(
        backward_kernel,
        [low, part, part, part, part],
        space,
        (
            x_rows,
            gain,
            cotangent,
            first,
            second,
            normed_rows,
            enc_q,
            enc_k,
            enc_v,
            enc_p,
            enc_ctx,
            order(mid_bit, low_bit),
            order(low_bit, mid_bit),
        ),
        28 * rows * DE * DE,
    )

    def added(former, latter):
        return (former.astype(jnp.float32) + latter.astype(jnp.float32)).astype(jnp.bfloat16)

    def cut(keep, came):
        half = keep.shape[1] // 2
        return added(keep[:, :half], came[:, :half]), added(keep[:, half:], came[:, half:])

    came_a, came_b = swap(a_send, "enc", 1), swap(b_send, "enc", 1)
    hidden, a_keep, b_keep = lax.optimization_barrier((hidden, a_keep, b_keep))
    a_keep, a_send = cut(a_keep, came_a)
    b_keep, b_send = cut(b_keep, came_b)

    sibling = swap(encoded, "enc", 1)
    across = swap(encoded, "enc", 2)
    across_sibling = swap(encoded, "enc", 3)
    pieces = (encoded, sibling, across, across_sibling)
    owner = neighbour_ids // local_count
    place = (owner ^ enc_at) * local_count + neighbour_ids % local_count
    stretch_count = neighbour_ids.shape[0]
    tokens = [piece.reshape(local_count, R, DE) for piece in pieces]

    def chosen(at):
        value = tokens[0][0]
        for i in range(1, enc_count * local_count):
            value = jnp.where(at == i, tokens[i // local_count][i % local_count], value)
        return value

    last = jnp.concatenate([chosen(place[stretch_count - 1, i]) for i in range(K)], axis=0)
    earlier_rows = shifted(last, "seq", 1)
    hidden_f = hidden.astype(jnp.float32)
    inv_rms = lax.rsqrt(jnp.mean(hidden_f * hidden_f, axis=-1, keepdims=True) + EPS)
    normed = (hidden_f * inv_rms * dec_gain).astype(jnp.bfloat16)
    token_count, model_width = hidden.shape
    padded = jnp.concatenate(
        [
            jnp.zeros((1, model_width), jnp.bfloat16),
            normed,
            jnp.zeros((C - 1, model_width), jnp.bfloat16),
        ],
        axis=0,
    )
    queries = matmul(padded, cca_query).astype(jnp.bfloat16)
    queries, a_send, b_send = lax.optimization_barrier((queries, a_send, b_send))
    came_a, came_b = swap(a_send, "enc", 2), swap(b_send, "seq", 1)
    pool_count = enc_count * local_count
    in_order = pool_count + jnp.arange(K, dtype=jnp.int32).reshape(1, K)
    spots = jnp.concatenate([in_order, place.astype(jnp.int32)], axis=0)
    context = decode(spots, queries, cca_key, cca_value, (*pieces, earlier_rows))
    context, a_keep, b_keep = lax.optimization_barrier((context, a_keep, b_keep))
    a_keep, a_send = cut(a_keep, came_a)
    b_keep, b_send = cut(b_keep, came_b)
    context = context[1 : token_count + 1]
    position = (
        seq_at * token_count + jnp.arange(token_count, dtype=jnp.int32) + C
    ) % SEQ_LEN
    context = jnp.where((position >= C - 1)[:, None], context, jnp.zeros_like(context))
    context, a_send, b_send = lax.optimization_barrier((context, a_send, b_send))
    came_a, came_b = swap(a_send, "seq", 1), swap(b_send, "enc", 2)
    slice_width = cca_out.shape[1] // enc_count

    def column(source, distance):
        return project(source, cca_out, enc_at ^ distance, enc_count)

    far_sent = swap(column(context, 3), "enc", 1)
    far_sum = added(column(context, 2), far_sent)
    context, far_sum = lax.optimization_barrier((context, far_sum))
    landed = swap(far_sum, "enc", 2)
    near_sent = swap(column(context, 1), "enc", 1)
    near = column(context, 0)
    near, a_keep, b_keep = lax.optimization_barrier((near, a_keep, b_keep))
    held = jnp.concatenate([added(a_keep, came_a), added(b_keep, came_b)], axis=0).reshape(
        4, lines, own_rows, DE
    )
    total = held[:, 0].astype(jnp.float32)
    for step in range(1, lines):
        moved = [(i, (i + 2 * step) % seq_count) for i in range(seq_count)]
        total = total + lax.ppermute(held[:, step], "seq", moved).astype(jnp.float32)
    total = total / (local_count * enc_count * seq_count)
    branch = (
        near.astype(jnp.float32) + near_sent.astype(jnp.float32) + landed.astype(jnp.float32)
    )
    residual = lax.dynamic_slice_in_dim(hidden, enc_at * slice_width, slice_width, 1)
    mixed = (residual.astype(jnp.float32) + branch).astype(jnp.bfloat16)
    return (mixed, d_input.reshape(neighbours.shape), total[2], total[3], total[0], total[1])


def solution(mesh):
    return jax.shard_map(
        on_device,
        mesh=mesh,
        in_specs=(
            P("seq", None),
            P(),
            P(None, "enc"),
            P(None, "enc"),
            P(None, "enc"),
            P("enc", None),
            P("seq", "enc", None, None),
            P(),
            P("enc", None),
            P("enc", None),
            P("enc", None),
            P("enc", None),
            P("seq", "enc", None, None),
            P("seq", None),
        ),
        out_specs=(
            P("seq", "enc"),
            P("seq", "enc", None, None),
            P(("enc", "seq"), None),
            P(("enc", "seq"), None),
            P(("enc", "seq"), None),
            P(("enc", "seq"), None),
        ),
        check_vma=False,
    )
```

```python
import functools

import jax
import jax.numpy as jnp
from jax import lax
from jax.experimental import pallas as pl
from jax.experimental.pallas import tpu as pltpu
from jax.sharding import PartitionSpec as P

HD = 128
DE = 896
EHEADS = 14
EHD = 64
C = 64
R = 128
K = 2
SEQ_LEN = 2048


EPS = 1e-06


def shifted(value, axis, steps):
    count = lax.axis_size(axis)
    initial, last = (max(0, -steps), min(count, count - steps))
    return lax.ppermute(value, axis, [(source, source + steps) for source in range(initial, last)])


def matmul(former, latter):
    return jnp.dot(former, latter, preferred_element_type=jnp.float32)


def inner_rows(former, latter):
    return lax.dot_general(
        former, latter, (((0,), (0,)), ((), ())), preferred_element_type=jnp.float32
    )


def outer_cols(former, latter):
    return lax.dot_general(
        former, latter, (((1,), (1,)), ((), ())), preferred_element_type=jnp.float32
    )


def two_heads(block):
    low = lax.broadcasted_iota(jnp.int32, block.shape, 1) < EHD
    zero = jnp.zeros_like(block)
    return jnp.concatenate([jnp.where(low, block, zero), jnp.where(low, zero, block)], axis=0)


def join_heads(stacked):
    half = stacked.shape[0] // 2
    low = lax.broadcasted_iota(jnp.int32, (half, stacked.shape[1]), 1) < EHD
    return jnp.where(low, stacked[:half], stacked[half:])


def softmax(scores):
    powers = jnp.exp(scores - jnp.max(scores, axis=-1, keepdims=True))
    return powers / jnp.sum(powers, axis=-1, keepdims=True)


def units(rows):
    pairs = EHEADS * EHD // 128
    return [
        (n * pairs + h, slice(n * R, (n + 1) * R), slice(h * 128, (h + 1) * 128))
        for n in range(rows // R)
        for h in range(pairs)
    ]


def forward_kernel(
    x_ref, gain_ref, qk_ref, vo_ref, enc_ref, normed_ref, q_ref, k_ref, v_ref, p_ref, ctx_ref
):
    x = x_ref[...].astype(jnp.float32)
    inv_rms = lax.rsqrt(jnp.mean(x * x, axis=-1, keepdims=True) + EPS)
    normed_ref[...] = (x * inv_rms * gain_ref[...]).astype(jnp.bfloat16)
    normed = normed_ref[...]
    q_ref[...] = matmul(normed, qk_ref[0]).astype(jnp.bfloat16)
    k_ref[...] = matmul(normed, qk_ref[1]).astype(jnp.bfloat16)
    v_ref[...] = matmul(normed, vo_ref[0]).astype(jnp.bfloat16)
    for at, rows, lanes in units(x_ref.shape[0]):
        scores = outer_cols(two_heads(q_ref[rows, lanes]), k_ref[rows, lanes]) * EHD ** (-0.5)
        weight = softmax(scores)
        p_ref[at] = weight
        ctx_ref[rows, lanes] = join_heads(
            matmul(weight.astype(jnp.bfloat16), v_ref[rows, lanes])
        ).astype(jnp.bfloat16)
    enc_ref[...] = (
        x_ref[...].astype(jnp.float32) + matmul(ctx_ref[...], vo_ref[1])
    ).astype(jnp.bfloat16)


def backward_kernel(
    x_ref,
    gain_ref,
    cot_ref,
    qk_ref,
    vo_ref,
    normed_ref,
    q_ref,
    k_ref,
    v_ref,
    p_ref,
    ctx_ref,
    order_a_ref,
    order_b_ref,
    dx_ref,
    a_keep,
    a_send,
    b_keep,
    b_send,
    dctx,
    dq,
    dk,
    dv,
):
    half = a_keep.shape[1]

    def emit(which, keep, send, former, latter):
        keep[which] = matmul(former[:half], latter).astype(jnp.bfloat16)
        send[which] = matmul(former[half:], latter).astype(jnp.bfloat16)

    dctx[...] = outer_cols(cot_ref[...], vo_ref[1]).astype(jnp.bfloat16)
    for at, rows, lanes in units(x_ref.shape[0]):
        d_context = two_heads(dctx[rows, lanes])
        weight = p_ref[at]
        d_p = outer_cols(d_context, v_ref[rows, lanes])
        dv[rows, lanes] = inner_rows(weight.astype(jnp.bfloat16), d_context).astype(jnp.bfloat16)
        d_s = (
            weight
            * (d_p - jnp.sum(d_p * weight, axis=-1, keepdims=True))
            * EHD ** (-0.5)
        ).astype(jnp.bfloat16)
        dq[rows, lanes] = join_heads(matmul(d_s, k_ref[rows, lanes])).astype(jnp.bfloat16)
        dk[rows, lanes] = inner_rows(d_s, two_heads(q_ref[rows, lanes])).astype(jnp.bfloat16)
    rows_a = outer_cols(order_a_ref[...], normed_ref[...]).astype(jnp.bfloat16)
    emit(0, a_keep, a_send, rows_a, dv[...])
    rows_o = outer_cols(order_a_ref[...], ctx_ref[...]).astype(jnp.bfloat16)
    emit(1, a_keep, a_send, rows_o, cot_ref[...])
    rows_b = outer_cols(order_b_ref[...], normed_ref[...]).astype(jnp.bfloat16)
    emit(0, b_keep, b_send, rows_b, dq[...])
    emit(1, b_keep, b_send, rows_b, dk[...])
    d_normed = (
        outer_cols(dq[...], qk_ref[0])
        + outer_cols(dk[...], qk_ref[1])
        + outer_cols(dv[...], vo_ref[0])
    )
    scaled = d_normed * gain_ref[...]
    x = x_ref[...].astype(jnp.float32)
    inv_rms = lax.rsqrt(jnp.mean(x * x, axis=-1, keepdims=True) + EPS)
    d_rows = inv_rms * scaled - x * inv_rms**3 * jnp.mean(x * scaled, axis=-1, keepdims=True)
    dx_ref[...] = (cot_ref[...].astype(jnp.float32) + d_rows).astype(jnp.bfloat16)


HEADS_STEP = 2


def decode_kernel(place_ref, q_ref, wk_ref, wv_ref, *refs):
    pieces, (ctx_ref, kv) = refs[:-2], refs[-2:]
    weights = jnp.concatenate([wk_ref[...], wv_ref[...]], axis=1)
    rows = pieces[0].shape[0]
    for at, piece in enumerate(pieces):
        kv[at * rows : (at + 1) * rows, :] = matmul(piece[...], weights).astype(jnp.bfloat16)
    groups = q_ref.shape[0] // C
    for head in range(HEADS_STEP):
        lanes = slice(head * HD, (head + 1) * HD)
        value_lanes = slice((HEADS_STEP + head) * HD, (HEADS_STEP + head + 1) * HD)
        scores, spots = [], []
        for group in range(groups):
            query = q_ref[group * C : (group + 1) * C, lanes]
            spot = [pl.ds(pl.multiple_of(place_ref[group, i] * R, R), R) for i in range(K)]
            scores.append(
                jnp.concatenate([outer_cols(query, kv[rows, lanes]) for rows in spot], axis=1)
            )
            spots.append(spot)
        weight = softmax(jnp.concatenate(scores, axis=0) * HD ** (-0.5)).astype(jnp.bfloat16)
        for group in range(groups):
            part = weight[group * C : (group + 1) * C]
            total = matmul(part[:, :R], kv[spots[group][0], value_lanes])
            for i in range(1, K):
                total = total + matmul(
                    part[:, i * R : (i + 1) * R], kv[spots[group][i], value_lanes]
                )
            ctx_ref[group * C : (group + 1) * C, lanes] = total.astype(jnp.bfloat16)


LIMIT = 60 * 1024 * 1024
SMALL_LIMIT = 24 * 1024 * 1024


def decode(place, queries, key_weight, value_weight, pieces):
    count, width = queries.shape
    whole = [pl.BlockSpec(piece.shape, lambda h: (0, 0)) for piece in pieces]
    rows = sum(piece.shape[0] for piece in pieces)
    column = lambda h: (0, h)
    flops = 2 * rows * DE * 2 * width + 4 * count * K * R * width
    return pl.pallas_call(
        decode_kernel,
        grid=(width // (HEADS_STEP * HD),),
        out_shape=jax.ShapeDtypeStruct((count, width), jnp.bfloat16),
        in_specs=[
            pl.BlockSpec(memory_space=pltpu.SMEM),
            pl.BlockSpec((count, HEADS_STEP * HD), column),
            pl.BlockSpec((DE, HEADS_STEP * HD), column),
            pl.BlockSpec((DE, HEADS_STEP * HD), column),
        ]
        + whole,
        out_specs=pl.BlockSpec((count, HEADS_STEP * HD), column),
        scratch_shapes=[pltpu.VMEM((rows, 2 * HEADS_STEP * HD), jnp.bfloat16)],
        compiler_params=pltpu.CompilerParams(vmem_limit_bytes=SMALL_LIMIT),
        cost_estimate=pl.CostEstimate(
            flops=2 * flops, bytes_accessed=rows * DE * 2 + 4 * DE * width, transcendentals=0
        ),
    )(place, queries, key_weight, value_weight, *pieces)


def one_call(kernel, outs, scratch, args, flops):
    vmem = pl.BlockSpec(memory_space=pltpu.VMEM)
    size = sum(a.size * a.dtype.itemsize for a in (*args, *outs))
    return pl.pallas_call(
        kernel,
        out_shape=outs,
        in_specs=[vmem] * len(args),
        out_specs=[vmem] * len(outs),
        scratch_shapes=scratch,
        compiler_params=pltpu.CompilerParams(vmem_limit_bytes=LIMIT),
        cost_estimate=pl.CostEstimate(flops=flops, bytes_accessed=size, transcendentals=0),
    )(*args)


def swap(value, axis, distance):
    count = lax.axis_size(axis)
    return lax.ppermute(value, axis, [(i, i ^ distance) for i in range(count)])


def gather_kernel(q_ref, k_ref, v_ref, o_ref, qk_ref, vo_ref, local_sem, send_sem, recv_sem):
    enc_at, seq_at = lax.axis_index("enc"), lax.axis_index("seq")
    pair = seq_at % 2
    sibling = (enc_at + 1 - 2 * (enc_at % 2), seq_at)
    across = ((enc_at + 2) % 4, seq_at)
    beside = (enc_at, seq_at + 1 - 2 * pair)
    height = q_ref.shape[0]
    half = height // 2
    barrier = pltpu.get_barrier_semaphore()
    for other in (sibling, across, beside):
        pl.semaphore_signal(barrier, inc=1, device_id=other, device_id_type=pl.DeviceIdType.MESH)
    pl.semaphore_wait(barrier, 3)

    def place(which, start, count):
        out = (qk_ref, vo_ref)[which // 2]
        return out.at[which % 2, pl.ds(pl.multiple_of(start, 16), count)]

    def send(kind, which, source, target, other):
        copy = pltpu.make_async_remote_copy(
            src_ref=source,
            dst_ref=target,
            send_sem=send_sem.at[kind, which],
            recv_sem=recv_sem.at[kind, which],
            device_id=other,
            device_id_type=pl.DeviceIdType.MESH,
        )
        copy.start()
        return copy

    blocks = (q_ref, k_ref, v_ref, o_ref)
    far = ((enc_at + 2) % 4) * height
    mine = enc_at * height
    copies, crossing, beside_copies = [], [], []
    for which, block in enumerate(blocks):
        rows = pl.ds(pl.multiple_of(pair * half, 16), half)
        crossing.append(
            send(0, which, block.at[rows], place(which, mine + pair * half, half), across)
        )
    for which, block in enumerate(blocks):
        copies.append(send(1, which, block, place(which, mine, height), sibling))
    locals_ = []
    for which, block in enumerate(blocks):
        copy = pltpu.make_async_copy(block, place(which, mine, height), local_sem.at[which])
        copy.start()
        locals_.append(copy)
    for which in range(4):
        crossing[which].wait_recv()
        landed = place(which, far + pair * half, half)
        beside_copies.append(send(2, which, landed, landed, beside))
        copies.append(send(3, which, landed, landed, sibling))
    for which in range(4):
        beside_copies[which].wait_recv()
        landed = place(which, far + (1 - pair) * half, half)
        copies.append(send(4, which, landed, landed, sibling))
    for copy in crossing + beside_copies:
        copy.wait_send()
    for copy in copies:
        copy.wait()
    for copy in locals_:
        copy.wait()


def gather_weights(blocks, count):
    height, width = blocks[0].shape
    out = jax.ShapeDtypeStruct((2, count * height, width), blocks[0].dtype)
    anywhere = pl.BlockSpec(memory_space=pltpu.HBM)
    return pl.pallas_call(
        gather_kernel,
        out_shape=[out, out],
        in_specs=[anywhere] * 4,
        out_specs=[anywhere] * 2,
        scratch_shapes=[
            pltpu.SemaphoreType.DMA((4,)),
            pltpu.SemaphoreType.DMA((5, 4)),
            pltpu.SemaphoreType.DMA((5, 4)),
        ],
        compiler_params=pltpu.CompilerParams(
            collective_id=0, has_side_effects=True, vmem_limit_bytes=LIMIT
        ),
    )(*blocks)


def choose_kernel(place_ref, *refs):
    pieces, out_ref = refs[:-1], refs[-1]
    tiles = pieces[0].shape[0] // R
    for at in range(K):
        for i in range(len(pieces) * tiles):

            @pl.when(place_ref[place_ref.shape[0] - 1, at] == i)
            def _():
                start = i % tiles * R
                out_ref[at * R : (at + 1) * R, :] = pieces[i // tiles][start : start + R, :]


def choose(place, pieces):
    vmem = pl.BlockSpec(memory_space=pltpu.VMEM)
    return pl.pallas_call(
        choose_kernel,
        out_shape=jax.ShapeDtypeStruct((K * R, pieces[0].shape[1]), pieces[0].dtype),
        in_specs=[pl.BlockSpec(memory_space=pltpu.SMEM)] + [vmem] * len(pieces),
        out_specs=vmem,
        compiler_params=pltpu.CompilerParams(vmem_limit_bytes=SMALL_LIMIT),
    )(place, *pieces)


def shares_kernel(a_keep, a_came, b_keep, b_came, *outs):
    rows = outs[0].shape[1]
    for pair, (keep, came) in enumerate(((a_keep, a_came), (b_keep, b_came))):
        for which in range(2):
            total = keep[which].astype(jnp.float32) + came[which].astype(jnp.float32)
            for at, out_ref in enumerate(outs):
                out_ref[2 * pair + which] = total[at * rows : (at + 1) * rows].astype(
                    jnp.bfloat16
                )


def shares(a_keep, a_came, b_keep, b_came, count):
    vmem = pl.BlockSpec(memory_space=pltpu.VMEM)
    _, rows, width = a_keep.shape
    out = jax.ShapeDtypeStruct((4, rows // count, width), jnp.bfloat16)
    return pl.pallas_call(
        shares_kernel,
        out_shape=[out] * count,
        in_specs=[vmem] * 4,
        out_specs=[vmem] * count,
        compiler_params=pltpu.CompilerParams(vmem_limit_bytes=SMALL_LIMIT),
    )(a_keep, a_came, b_keep, b_came)


def finish_kernel(scale, *refs):
    parts, outs = refs[:-4], refs[-4:]
    for which, out_ref in enumerate(outs):
        total = parts[0][which].astype(jnp.float32)
        for part in parts[1:]:
            total = total + part[which].astype(jnp.float32)
        out_ref[...] = total * scale


def finish(parts, scale):
    vmem = pl.BlockSpec(memory_space=pltpu.VMEM)
    return pl.pallas_call(
        functools.partial(finish_kernel, scale),
        out_shape=[jax.ShapeDtypeStruct(parts[0].shape[1:], jnp.float32)] * 4,
        in_specs=[vmem] * len(parts),
        out_specs=[vmem] * 4,
        compiler_params=pltpu.CompilerParams(vmem_limit_bytes=SMALL_LIMIT),
    )(*parts)


def project_kernel(_, context_ref, weight_ref, out_ref):
    out_ref[...] = matmul(context_ref[...], weight_ref[...]).astype(jnp.bfloat16)


def project(context, weight, which, count):
    tokens, depth = context.shape
    width = weight.shape[1] // count
    steps = 2
    tile = width // steps
    return pl.pallas_call(
        project_kernel,
        out_shape=jax.ShapeDtypeStruct((tokens, width), jnp.bfloat16),
        grid_spec=pltpu.PrefetchScalarGridSpec(
            num_scalar_prefetch=1,
            grid=(steps,),
            in_specs=[
                pl.BlockSpec((tokens, depth), lambda i, at: (0, 0)),
                pl.BlockSpec((depth, tile), lambda i, at: (0, at[0] * steps + i)),
            ],
            out_specs=pl.BlockSpec((tokens, tile), lambda i, at: (0, i)),
        ),
        compiler_params=pltpu.CompilerParams(vmem_limit_bytes=SMALL_LIMIT),
        cost_estimate=pl.CostEstimate(
            flops=2 * tokens * depth * width, bytes_accessed=2 * depth * width, transcendentals=0
        ),
    )(which.astype(jnp.int32).reshape(1), context, weight)


def on_device(
    hidden,
    dec_gain,
    cca_query,
    cca_key,
    cca_value,
    cca_out,
    neighbours,
    enc_gain,
    enc_query,
    enc_key,
    enc_value,
    enc_output,
    enc_cotangent,
    neighbour_ids,
):
    enc_count, seq_count = lax.axis_size("enc"), lax.axis_size("seq")
    enc_at, seq_at = lax.axis_index("enc"), lax.axis_index("seq")
    core, chip, pair, line = enc_at % 2, enc_at // 2, seq_at % 2, seq_at // 2
    lines = seq_count // 2
    first, second = gather_weights((enc_query, enc_key, enc_value, enc_output), enc_count)
    local_count = neighbours.shape[1]
    rows = local_count * R
    x_rows = neighbours.reshape(rows, DE)
    cotangent = enc_cotangent.reshape(rows, DE)
    gain = enc_gain.reshape(1, DE)
    low = jax.ShapeDtypeStruct((rows, DE), jnp.bfloat16)
    soft = jax.ShapeDtypeStruct((rows // R * (DE // 128), 2 * R, R), jnp.float32)
    encoded, normed_rows, enc_q, enc_k, enc_v, enc_p, enc_ctx = one_call(
        forward_kernel,
        [low, low, low, low, low, soft, low],
        [],
        (x_rows, gain, first, second),
        12 * rows * DE * DE,
    )
    own_rows = DE // (enc_count * seq_count)
    target = jnp.arange(DE, dtype=jnp.int32)
    inner, block = target % own_rows, target // own_rows
    ahead = (line + block % lines) % lines
    low_bit, mid_bit, top_bit = (
        block // lines % 2,
        block // lines // 2 % 2,
        block // lines // 4,
    )

    def order(chip_bit, pair_bit):
        device = ((chip ^ chip_bit) * 2 + (core ^ top_bit)) * seq_count + ahead * 2 + (
            pair ^ pair_bit
        )
        return (target[None, :] == (device * own_rows + inner)[:, None]).astype(jnp.bfloat16)

    part = jax.ShapeDtypeStruct((2, DE // 2, DE), jnp.bfloat16)
    space = [pltpu.VMEM((rows, DE), jnp.bfloat16)] * 4
    d_input, a_keep, a_send, b_keep, b_send = one_call(
        backward_kernel,
        [low, part, part, part, part],
        space,
        (
            x_rows,
            gain,
            cotangent,
            first,
            second,
            normed_rows,
            enc_q,
            enc_k,
            enc_v,
            enc_p,
            enc_ctx,
            order(mid_bit, low_bit),
            order(low_bit, mid_bit),
        ),
        28 * rows * DE * DE,
    )

    def added(former, latter):
        return (former.astype(jnp.float32) + latter.astype(jnp.float32)).astype(jnp.bfloat16)

    def cut(keep, came):
        half = keep.shape[1] // 2
        return added(keep[:, :half], came[:, :half]), added(keep[:, half:], came[:, half:])

    came_a, came_b = swap(a_send, "enc", 1), swap(b_send, "enc", 1)
    sibling = swap(encoded, "enc", 1)
    across = swap(encoded, "enc", 2)
    across_sibling = swap(encoded, "enc", 3)
    pieces = (encoded, sibling, across, across_sibling)
    owner = neighbour_ids // local_count
    place = (owner ^ enc_at) * local_count + neighbour_ids % local_count
    stretch_count = neighbour_ids.shape[0]
    place = place.astype(jnp.int32)
    last = choose(place, pieces)
    hidden, a_keep, b_keep, last = lax.optimization_barrier((hidden, a_keep, b_keep, last))
    earlier_rows = shifted(last, "seq", 1)
    hidden_f = hidden.astype(jnp.float32)
    inv_rms = lax.rsqrt(jnp.mean(hidden_f * hidden_f, axis=-1, keepdims=True) + EPS)
    normed = (hidden_f * inv_rms * dec_gain).astype(jnp.bfloat16)
    token_count, model_width = hidden.shape
    padded = jnp.concatenate(
        [
            jnp.zeros((1, model_width), jnp.bfloat16),
            normed,
            jnp.zeros((C - 1, model_width), jnp.bfloat16),
        ],
        axis=0,
    )
    queries = matmul(padded, cca_query).astype(jnp.bfloat16)
    queries, a_keep, b_keep = lax.optimization_barrier((queries, a_keep, b_keep))
    a_keep, a_send = cut(a_keep, came_a)
    b_keep, b_send = cut(b_keep, came_b)
    queries, a_send, b_send = lax.optimization_barrier((queries, a_send, b_send))
    came_a, came_b = swap(a_send, "enc", 2), swap(b_send, "seq", 1)
    pool_count = enc_count * local_count
    in_order = pool_count + jnp.arange(K, dtype=jnp.int32).reshape(1, K)
    spots = jnp.concatenate([in_order, place], axis=0)
    context = decode(spots, queries, cca_key, cca_value, (*pieces, earlier_rows))
    context, a_keep, b_keep = lax.optimization_barrier((context, a_keep, b_keep))
    a_keep, a_send = cut(a_keep, came_a)
    b_keep, b_send = cut(b_keep, came_b)
    context = context[1 : token_count + 1]
    position = (
        seq_at * token_count + jnp.arange(token_count, dtype=jnp.int32) + C
    ) % SEQ_LEN
    context = jnp.where((position >= C - 1)[:, None], context, jnp.zeros_like(context))
    context, a_send, b_send = lax.optimization_barrier((context, a_send, b_send))
    came_a, came_b = swap(a_send, "seq", 1), swap(b_send, "enc", 2)
    slice_width = cca_out.shape[1] // enc_count

    def column(source, distance):
        return project(source, cca_out, enc_at ^ distance, enc_count)

    far_sent = swap(column(context, 3), "enc", 1)
    far_sum = added(column(context, 2), far_sent)
    context, far_sum = lax.optimization_barrier((context, far_sum))
    landed = swap(far_sum, "enc", 2)
    near_sent = swap(column(context, 1), "enc", 1)
    near = column(context, 0)
    near, a_keep, b_keep = lax.optimization_barrier((near, a_keep, b_keep))
    held = shares(a_keep, came_a, b_keep, came_b, lines)
    parts = [held[0]]
    for step in range(1, lines):
        moved = [(i, (i + 2 * step) % seq_count) for i in range(seq_count)]
        parts.append(lax.ppermute(held[step], "seq", moved))
    total = finish(parts, 1.0 / (local_count * enc_count * seq_count))
    branch = (
        near.astype(jnp.float32) + near_sent.astype(jnp.float32) + landed.astype(jnp.float32)
    )
    residual = lax.dynamic_slice_in_dim(hidden, enc_at * slice_width, slice_width, 1)
    mixed = (residual.astype(jnp.float32) + branch).astype(jnp.bfloat16)
    return (mixed, d_input.reshape(neighbours.shape), total[2], total[3], total[0], total[1])


def solution(mesh):
    return jax.shard_map(
        on_device,
        mesh=mesh,
        in_specs=(
            P("seq", None),
            P(),
            P(None, "enc"),
            P(None, "enc"),
            P(None, "enc"),
            P("enc", None),
            P("seq", "enc", None, None),
            P(),
            P("enc", None),
            P("enc", None),
            P("enc", None),
            P("enc", None),
            P("seq", "enc", None, None),
            P("seq", None),
        ),
        out_specs=(
            P("seq", "enc"),
            P("seq", "enc", None, None),
            P(("enc", "seq"), None),
            P(("enc", "seq"), None),
            P(("enc", "seq"), None),
            P(("enc", "seq"), None),
        ),
        check_vma=False,
    )
```

```python
import functools

import jax
import jax.numpy as jnp
from jax import lax
from jax.experimental import pallas as pl
from jax.experimental.pallas import tpu as pltpu
from jax.sharding import PartitionSpec as P

HD = 128
DE = 896
EHEADS = 14
EHD = 64
C = 64
R = 128
K = 2
SEQ_LEN = 2048


EPS = 1e-06


def shifted(value, axis, steps):
    count = lax.axis_size(axis)
    initial, last = (max(0, -steps), min(count, count - steps))
    return lax.ppermute(value, axis, [(source, source + steps) for source in range(initial, last)])


def matmul(former, latter):
    return jnp.dot(former, latter, preferred_element_type=jnp.float32)


def inner_rows(former, latter):
    return lax.dot_general(
        former, latter, (((0,), (0,)), ((), ())), preferred_element_type=jnp.float32
    )


def outer_cols(former, latter):
    return lax.dot_general(
        former, latter, (((1,), (1,)), ((), ())), preferred_element_type=jnp.float32
    )


def two_heads(block):
    low = lax.broadcasted_iota(jnp.int32, block.shape, 1) < EHD
    zero = jnp.zeros_like(block)
    return jnp.concatenate([jnp.where(low, block, zero), jnp.where(low, zero, block)], axis=0)


def join_heads(stacked):
    half = stacked.shape[0] // 2
    low = lax.broadcasted_iota(jnp.int32, (half, stacked.shape[1]), 1) < EHD
    return jnp.where(low, stacked[:half], stacked[half:])


def softmax(scores):
    powers = jnp.exp(scores - jnp.max(scores, axis=-1, keepdims=True))
    return powers / jnp.sum(powers, axis=-1, keepdims=True)


def units(rows):
    pairs = EHEADS * EHD // 128
    return [
        (n * pairs + h, slice(n * R, (n + 1) * R), slice(h * 128, (h + 1) * 128))
        for n in range(rows // R)
        for h in range(pairs)
    ]


def forward_kernel(
    x_ref, gain_ref, qk_ref, vo_ref, enc_ref, normed_ref, q_ref, k_ref, v_ref, p_ref, ctx_ref
):
    x = x_ref[...].astype(jnp.float32)
    inv_rms = lax.rsqrt(jnp.mean(x * x, axis=-1, keepdims=True) + EPS)
    normed_ref[...] = (x * inv_rms * gain_ref[...]).astype(jnp.bfloat16)
    normed = normed_ref[...]
    q_ref[...] = matmul(normed, qk_ref[0]).astype(jnp.bfloat16)
    k_ref[...] = matmul(normed, qk_ref[1]).astype(jnp.bfloat16)
    v_ref[...] = matmul(normed, vo_ref[0]).astype(jnp.bfloat16)
    for at, rows, lanes in units(x_ref.shape[0]):
        scores = outer_cols(two_heads(q_ref[rows, lanes]), k_ref[rows, lanes]) * EHD ** (-0.5)
        weight = softmax(scores)
        p_ref[at] = weight
        ctx_ref[rows, lanes] = join_heads(
            matmul(weight.astype(jnp.bfloat16), v_ref[rows, lanes])
        ).astype(jnp.bfloat16)
    enc_ref[...] = (
        x_ref[...].astype(jnp.float32) + matmul(ctx_ref[...], vo_ref[1])
    ).astype(jnp.bfloat16)


def backward_kernel(
    x_ref,
    gain_ref,
    cot_ref,
    qk_ref,
    vo_ref,
    normed_ref,
    q_ref,
    k_ref,
    v_ref,
    p_ref,
    ctx_ref,
    order_a_ref,
    order_b_ref,
    dx_ref,
    a_keep,
    a_send,
    b_keep,
    b_send,
    dctx,
    dq,
    dk,
    dv,
):
    half = a_keep.shape[1]

    def emit(which, keep, send, former, latter):
        keep[which] = matmul(former[:half], latter).astype(jnp.bfloat16)
        send[which] = matmul(former[half:], latter).astype(jnp.bfloat16)

    dctx[...] = outer_cols(cot_ref[...], vo_ref[1]).astype(jnp.bfloat16)
    for at, rows, lanes in units(x_ref.shape[0]):
        d_context = two_heads(dctx[rows, lanes])
        weight = p_ref[at]
        d_p = outer_cols(d_context, v_ref[rows, lanes])
        dv[rows, lanes] = inner_rows(weight.astype(jnp.bfloat16), d_context).astype(jnp.bfloat16)
        d_s = (
            weight
            * (d_p - jnp.sum(d_p * weight, axis=-1, keepdims=True))
            * EHD ** (-0.5)
        ).astype(jnp.bfloat16)
        dq[rows, lanes] = join_heads(matmul(d_s, k_ref[rows, lanes])).astype(jnp.bfloat16)
        dk[rows, lanes] = inner_rows(d_s, two_heads(q_ref[rows, lanes])).astype(jnp.bfloat16)
    rows_a = outer_cols(order_a_ref[...], normed_ref[...]).astype(jnp.bfloat16)
    emit(0, a_keep, a_send, rows_a, dv[...])
    rows_o = outer_cols(order_a_ref[...], ctx_ref[...]).astype(jnp.bfloat16)
    emit(1, a_keep, a_send, rows_o, cot_ref[...])
    rows_b = outer_cols(order_b_ref[...], normed_ref[...]).astype(jnp.bfloat16)
    emit(0, b_keep, b_send, rows_b, dq[...])
    emit(1, b_keep, b_send, rows_b, dk[...])
    d_normed = (
        outer_cols(dq[...], qk_ref[0])
        + outer_cols(dk[...], qk_ref[1])
        + outer_cols(dv[...], vo_ref[0])
    )
    scaled = d_normed * gain_ref[...]
    x = x_ref[...].astype(jnp.float32)
    inv_rms = lax.rsqrt(jnp.mean(x * x, axis=-1, keepdims=True) + EPS)
    d_rows = inv_rms * scaled - x * inv_rms**3 * jnp.mean(x * scaled, axis=-1, keepdims=True)
    dx_ref[...] = (cot_ref[...].astype(jnp.float32) + d_rows).astype(jnp.bfloat16)


HEADS_STEP = 2


def decode_kernel(place_ref, q_ref, wk_ref, wv_ref, *refs):
    pieces, (ctx_ref, kv) = refs[:-2], refs[-2:]
    weights = jnp.concatenate([wk_ref[...], wv_ref[...]], axis=1)
    rows = pieces[0].shape[0]
    for at, piece in enumerate(pieces):
        kv[at * rows : (at + 1) * rows, :] = matmul(piece[...], weights).astype(jnp.bfloat16)
    groups = q_ref.shape[0] // C
    for head in range(HEADS_STEP):
        lanes = slice(head * HD, (head + 1) * HD)
        value_lanes = slice((HEADS_STEP + head) * HD, (HEADS_STEP + head + 1) * HD)
        scores, spots = [], []
        for group in range(groups):
            query = q_ref[group * C : (group + 1) * C, lanes]
            spot = [pl.ds(pl.multiple_of(place_ref[group, i] * R, R), R) for i in range(K)]
            scores.append(
                jnp.concatenate([outer_cols(query, kv[rows, lanes]) for rows in spot], axis=1)
            )
            spots.append(spot)
        weight = softmax(jnp.concatenate(scores, axis=0) * HD ** (-0.5)).astype(jnp.bfloat16)
        for group in range(groups):
            part = weight[group * C : (group + 1) * C]
            total = matmul(part[:, :R], kv[spots[group][0], value_lanes])
            for i in range(1, K):
                total = total + matmul(
                    part[:, i * R : (i + 1) * R], kv[spots[group][i], value_lanes]
                )
            ctx_ref[group * C : (group + 1) * C, lanes] = total.astype(jnp.bfloat16)


LIMIT = 60 * 1024 * 1024
SMALL_LIMIT = 24 * 1024 * 1024


def decode(place, queries, key_weight, value_weight, pieces):
    count, width = queries.shape
    whole = [pl.BlockSpec(piece.shape, lambda h: (0, 0)) for piece in pieces]
    rows = sum(piece.shape[0] for piece in pieces)
    column = lambda h: (0, h)
    flops = 2 * rows * DE * 2 * width + 4 * count * K * R * width
    return pl.pallas_call(
        decode_kernel,
        grid=(width // (HEADS_STEP * HD),),
        out_shape=jax.ShapeDtypeStruct((count, width), jnp.bfloat16),
        in_specs=[
            pl.BlockSpec(memory_space=pltpu.SMEM),
            pl.BlockSpec((count, HEADS_STEP * HD), column),
            pl.BlockSpec((DE, HEADS_STEP * HD), column),
            pl.BlockSpec((DE, HEADS_STEP * HD), column),
        ]
        + whole,
        out_specs=pl.BlockSpec((count, HEADS_STEP * HD), column),
        scratch_shapes=[pltpu.VMEM((rows, 2 * HEADS_STEP * HD), jnp.bfloat16)],
        compiler_params=pltpu.CompilerParams(vmem_limit_bytes=SMALL_LIMIT),
        cost_estimate=pl.CostEstimate(
            flops=2 * flops, bytes_accessed=rows * DE * 2 + 4 * DE * width, transcendentals=0
        ),
    )(place, queries, key_weight, value_weight, *pieces)


def one_call(kernel, outs, scratch, args, flops):
    vmem = pl.BlockSpec(memory_space=pltpu.VMEM)
    size = sum(a.size * a.dtype.itemsize for a in (*args, *outs))
    return pl.pallas_call(
        kernel,
        out_shape=outs,
        in_specs=[vmem] * len(args),
        out_specs=[vmem] * len(outs),
        scratch_shapes=scratch,
        compiler_params=pltpu.CompilerParams(vmem_limit_bytes=LIMIT),
        cost_estimate=pl.CostEstimate(flops=flops, bytes_accessed=size, transcendentals=0),
    )(*args)


def swap(value, axis, distance):
    count = lax.axis_size(axis)
    return lax.ppermute(value, axis, [(i, i ^ distance) for i in range(count)])


def gather_kernel(q_ref, k_ref, v_ref, o_ref, qk_ref, vo_ref, local_sem, send_sem, recv_sem):
    enc_at, seq_at = lax.axis_index("enc"), lax.axis_index("seq")
    pair = seq_at % 2
    sibling = (enc_at + 1 - 2 * (enc_at % 2), seq_at)
    across = ((enc_at + 2) % 4, seq_at)
    beside = (enc_at, seq_at + 1 - 2 * pair)
    height = q_ref.shape[0]
    half = height // 2
    barrier = pltpu.get_barrier_semaphore()
    for other in (sibling, across, beside):
        pl.semaphore_signal(barrier, inc=1, device_id=other, device_id_type=pl.DeviceIdType.MESH)
    pl.semaphore_wait(barrier, 3)

    def place(which, start, count):
        out = (qk_ref, vo_ref)[which // 2]
        return out.at[which % 2, pl.ds(pl.multiple_of(start, 16), count)]

    def send(kind, which, source, target, other):
        copy = pltpu.make_async_remote_copy(
            src_ref=source,
            dst_ref=target,
            send_sem=send_sem.at[kind, which],
            recv_sem=recv_sem.at[kind, which],
            device_id=other,
            device_id_type=pl.DeviceIdType.MESH,
        )
        copy.start()
        return copy

    blocks = (q_ref, k_ref, v_ref, o_ref)
    far = ((enc_at + 2) % 4) * height
    mine = enc_at * height
    copies, crossing, beside_copies = [], [], []
    for which, block in enumerate(blocks):
        rows = pl.ds(pl.multiple_of(pair * half, 16), half)
        crossing.append(
            send(0, which, block.at[rows], place(which, mine + pair * half, half), across)
        )
    for which, block in enumerate(blocks):
        copies.append(send(1, which, block, place(which, mine, height), sibling))
    locals_ = []
    for which, block in enumerate(blocks):
        copy = pltpu.make_async_copy(block, place(which, mine, height), local_sem.at[which])
        copy.start()
        locals_.append(copy)
    for which in range(4):
        crossing[which].wait_recv()
        landed = place(which, far + pair * half, half)
        beside_copies.append(send(2, which, landed, landed, beside))
        copies.append(send(3, which, landed, landed, sibling))
    for which in range(4):
        beside_copies[which].wait_recv()
        landed = place(which, far + (1 - pair) * half, half)
        copies.append(send(4, which, landed, landed, sibling))
    for copy in crossing + beside_copies:
        copy.wait_send()
    for copy in copies:
        copy.wait()
    for copy in locals_:
        copy.wait()


def gather_weights(blocks, count):
    height, width = blocks[0].shape
    out = jax.ShapeDtypeStruct((2, count * height, width), blocks[0].dtype)
    resident = pl.BlockSpec(memory_space=pltpu.VMEM)
    return pl.pallas_call(
        gather_kernel,
        out_shape=[out, out],
        in_specs=[resident] * 4,
        out_specs=[resident] * 2,
        scratch_shapes=[
            pltpu.SemaphoreType.DMA((4,)),
            pltpu.SemaphoreType.DMA((5, 4)),
            pltpu.SemaphoreType.DMA((5, 4)),
        ],
        compiler_params=pltpu.CompilerParams(
            collective_id=0, has_side_effects=True, vmem_limit_bytes=LIMIT
        ),
    )(*blocks)


def choose_kernel(place_ref, *refs):
    pieces, out_ref = refs[:-1], refs[-1]
    tiles = pieces[0].shape[0] // R
    for at in range(K):
        for i in range(len(pieces) * tiles):

            @pl.when(place_ref[place_ref.shape[0] - 1, at] == i)
            def _():
                start = i % tiles * R
                out_ref[at * R : (at + 1) * R, :] = pieces[i // tiles][start : start + R, :]


def choose(place, pieces):
    vmem = pl.BlockSpec(memory_space=pltpu.VMEM)
    return pl.pallas_call(
        choose_kernel,
        out_shape=jax.ShapeDtypeStruct((K * R, pieces[0].shape[1]), pieces[0].dtype),
        in_specs=[pl.BlockSpec(memory_space=pltpu.SMEM)] + [vmem] * len(pieces),
        out_specs=vmem,
        compiler_params=pltpu.CompilerParams(vmem_limit_bytes=SMALL_LIMIT),
    )(place, *pieces)


def shares_kernel(a_keep, a_came, b_keep, b_came, *outs):
    rows = outs[0].shape[1]
    for pair, (keep, came) in enumerate(((a_keep, a_came), (b_keep, b_came))):
        for which in range(2):
            total = keep[which].astype(jnp.float32) + came[which].astype(jnp.float32)
            for at, out_ref in enumerate(outs):
                out_ref[2 * pair + which] = total[at * rows : (at + 1) * rows].astype(
                    jnp.bfloat16
                )


def shares(a_keep, a_came, b_keep, b_came, count):
    vmem = pl.BlockSpec(memory_space=pltpu.VMEM)
    _, rows, width = a_keep.shape
    out = jax.ShapeDtypeStruct((4, rows // count, width), jnp.bfloat16)
    return pl.pallas_call(
        shares_kernel,
        out_shape=[out] * count,
        in_specs=[vmem] * 4,
        out_specs=[vmem] * count,
        compiler_params=pltpu.CompilerParams(vmem_limit_bytes=SMALL_LIMIT),
    )(a_keep, a_came, b_keep, b_came)


def finish_kernel(scale, *refs):
    parts, outs = refs[:-4], refs[-4:]
    for which, out_ref in enumerate(outs):
        total = parts[0][which].astype(jnp.float32)
        for part in parts[1:]:
            total = total + part[which].astype(jnp.float32)
        out_ref[...] = total * scale


def finish(parts, scale):
    vmem = pl.BlockSpec(memory_space=pltpu.VMEM)
    return pl.pallas_call(
        functools.partial(finish_kernel, scale),
        out_shape=[jax.ShapeDtypeStruct(parts[0].shape[1:], jnp.float32)] * 4,
        in_specs=[vmem] * len(parts),
        out_specs=[vmem] * 4,
        compiler_params=pltpu.CompilerParams(vmem_limit_bytes=SMALL_LIMIT),
    )(*parts)


def project_kernel(_, context_ref, weight_ref, out_ref):
    out_ref[...] = matmul(context_ref[...], weight_ref[...]).astype(jnp.bfloat16)


def project(context, weight, which, count):
    tokens, depth = context.shape
    width = weight.shape[1] // count
    steps = 2
    tile = width // steps
    return pl.pallas_call(
        project_kernel,
        out_shape=jax.ShapeDtypeStruct((tokens, width), jnp.bfloat16),
        grid_spec=pltpu.PrefetchScalarGridSpec(
            num_scalar_prefetch=1,
            grid=(steps,),
            in_specs=[
                pl.BlockSpec((tokens, depth), lambda i, at: (0, 0)),
                pl.BlockSpec((depth, tile), lambda i, at: (0, at[0] * steps + i)),
            ],
            out_specs=pl.BlockSpec((tokens, tile), lambda i, at: (0, i)),
        ),
        compiler_params=pltpu.CompilerParams(vmem_limit_bytes=SMALL_LIMIT),
        cost_estimate=pl.CostEstimate(
            flops=2 * tokens * depth * width, bytes_accessed=2 * depth * width, transcendentals=0
        ),
    )(which.astype(jnp.int32).reshape(1), context, weight)


def on_device(
    hidden,
    dec_gain,
    cca_query,
    cca_key,
    cca_value,
    cca_out,
    neighbours,
    enc_gain,
    enc_query,
    enc_key,
    enc_value,
    enc_output,
    enc_cotangent,
    neighbour_ids,
):
    enc_count, seq_count = lax.axis_size("enc"), lax.axis_size("seq")
    enc_at, seq_at = lax.axis_index("enc"), lax.axis_index("seq")
    core, chip, pair, line = enc_at % 2, enc_at // 2, seq_at % 2, seq_at // 2
    lines = seq_count // 2
    first, second = gather_weights((enc_query, enc_key, enc_value, enc_output), enc_count)
    local_count = neighbours.shape[1]
    rows = local_count * R
    x_rows = neighbours.reshape(rows, DE)
    cotangent = enc_cotangent.reshape(rows, DE)
    gain = enc_gain.reshape(1, DE)
    low = jax.ShapeDtypeStruct((rows, DE), jnp.bfloat16)
    soft = jax.ShapeDtypeStruct((rows // R * (DE // 128), 2 * R, R), jnp.float32)
    encoded, normed_rows, enc_q, enc_k, enc_v, enc_p, enc_ctx = one_call(
        forward_kernel,
        [low, low, low, low, low, soft, low],
        [],
        (x_rows, gain, first, second),
        12 * rows * DE * DE,
    )
    own_rows = DE // (enc_count * seq_count)
    target = jnp.arange(DE, dtype=jnp.int32)
    inner, block = target % own_rows, target // own_rows
    ahead = (line + block % lines) % lines
    low_bit, mid_bit, top_bit = (
        block // lines % 2,
        block // lines // 2 % 2,
        block // lines // 4,
    )

    def order(chip_bit, pair_bit):
        device = ((chip ^ chip_bit) * 2 + (core ^ top_bit)) * seq_count + ahead * 2 + (
            pair ^ pair_bit
        )
        return (target[None, :] == (device * own_rows + inner)[:, None]).astype(jnp.bfloat16)

    part = jax.ShapeDtypeStruct((2, DE // 2, DE), jnp.bfloat16)
    space = [pltpu.VMEM((rows, DE), jnp.bfloat16)] * 4
    d_input, a_keep, a_send, b_keep, b_send = one_call(
        backward_kernel,
        [low, part, part, part, part],
        space,
        (
            x_rows,
            gain,
            cotangent,
            first,
            second,
            normed_rows,
            enc_q,
            enc_k,
            enc_v,
            enc_p,
            enc_ctx,
            order(mid_bit, low_bit),
            order(low_bit, mid_bit),
        ),
        28 * rows * DE * DE,
    )

    def added(former, latter):
        return (former.astype(jnp.float32) + latter.astype(jnp.float32)).astype(jnp.bfloat16)

    def cut(keep, came):
        half = keep.shape[1] // 2
        return added(keep[:, :half], came[:, :half]), added(keep[:, half:], came[:, half:])

    came_a, came_b = swap(a_send, "enc", 1), swap(b_send, "enc", 1)
    sibling = swap(encoded, "enc", 1)
    across = swap(encoded, "enc", 2)
    across_sibling = swap(encoded, "enc", 3)
    pieces = (encoded, sibling, across, across_sibling)
    owner = neighbour_ids // local_count
    place = (owner ^ enc_at) * local_count + neighbour_ids % local_count
    stretch_count = neighbour_ids.shape[0]
    place = place.astype(jnp.int32)
    last = choose(place, pieces)
    hidden, a_keep, b_keep, last = lax.optimization_barrier((hidden, a_keep, b_keep, last))
    earlier_rows = shifted(last, "seq", 1)
    hidden_f = hidden.astype(jnp.float32)
    inv_rms = lax.rsqrt(jnp.mean(hidden_f * hidden_f, axis=-1, keepdims=True) + EPS)
    normed = (hidden_f * inv_rms * dec_gain).astype(jnp.bfloat16)
    token_count, model_width = hidden.shape
    padded = jnp.concatenate(
        [
            jnp.zeros((1, model_width), jnp.bfloat16),
            normed,
            jnp.zeros((C - 1, model_width), jnp.bfloat16),
        ],
        axis=0,
    )
    queries = matmul(padded, cca_query).astype(jnp.bfloat16)
    queries, a_keep, b_keep = lax.optimization_barrier((queries, a_keep, b_keep))
    a_keep, a_send = cut(a_keep, came_a)
    b_keep, b_send = cut(b_keep, came_b)
    queries, a_send, b_send = lax.optimization_barrier((queries, a_send, b_send))
    came_a, came_b = swap(a_send, "enc", 2), swap(b_send, "seq", 1)
    pool_count = enc_count * local_count
    in_order = pool_count + jnp.arange(K, dtype=jnp.int32).reshape(1, K)
    spots = jnp.concatenate([in_order, place], axis=0)
    context = decode(spots, queries, cca_key, cca_value, (*pieces, earlier_rows))
    context, a_keep, b_keep = lax.optimization_barrier((context, a_keep, b_keep))
    a_keep, a_send = cut(a_keep, came_a)
    b_keep, b_send = cut(b_keep, came_b)
    context = context[1 : token_count + 1]
    position = (
        seq_at * token_count + jnp.arange(token_count, dtype=jnp.int32) + C
    ) % SEQ_LEN
    context = jnp.where((position >= C - 1)[:, None], context, jnp.zeros_like(context))
    context, a_send, b_send = lax.optimization_barrier((context, a_send, b_send))
    came_a, came_b = swap(a_send, "seq", 1), swap(b_send, "enc", 2)
    slice_width = cca_out.shape[1] // enc_count

    def column(source, distance):
        return project(source, cca_out, enc_at ^ distance, enc_count)

    far_sent = swap(column(context, 3), "enc", 1)
    far_sum = added(column(context, 2), far_sent)
    context, far_sum = lax.optimization_barrier((context, far_sum))
    landed = swap(far_sum, "enc", 2)
    near_sent = swap(column(context, 1), "enc", 1)
    near = column(context, 0)
    near, a_keep, b_keep = lax.optimization_barrier((near, a_keep, b_keep))
    held = shares(a_keep, came_a, b_keep, came_b, lines)
    parts = [held[0]]
    for step in range(1, lines):
        moved = [(i, (i + 2 * step) % seq_count) for i in range(seq_count)]
        parts.append(lax.ppermute(held[step], "seq", moved))
    total = finish(parts, 1.0 / (local_count * enc_count * seq_count))
    branch = (
        near.astype(jnp.float32) + near_sent.astype(jnp.float32) + landed.astype(jnp.float32)
    )
    residual = lax.dynamic_slice_in_dim(hidden, enc_at * slice_width, slice_width, 1)
    mixed = (residual.astype(jnp.float32) + branch).astype(jnp.bfloat16)
    return (mixed, d_input.reshape(neighbours.shape), total[2], total[3], total[0], total[1])


def solution(mesh):
    return jax.shard_map(
        on_device,
        mesh=mesh,
        in_specs=(
            P("seq", None),
            P(),
            P(None, "enc"),
            P(None, "enc"),
            P(None, "enc"),
            P("enc", None),
            P("seq", "enc", None, None),
            P(),
            P("enc", None),
            P("enc", None),
            P("enc", None),
            P("enc", None),
            P("seq", "enc", None, None),
            P("seq", None),
        ),
        out_specs=(
            P("seq", "enc"),
            P("seq", "enc", None, None),
            P(("enc", "seq"), None),
            P(("enc", "seq"), None),
            P(("enc", "seq"), None),
            P(("enc", "seq"), None),
        ),
        check_vma=False,
    )
```
